256 devices in a mesh: sec: 16 (over x, y), op: 16 (over z, core).
Axes of the slice: x: 4, y: 4, z: 8, core: 2. Of those that a mesh axis runs over, the one named last changes fastest.
Arguments:
- wavefunction: bfloat16 [64, 256, 256], P('sec'), may hold values from -6 to 6
- sector_dims: int32 [64, 2], P('sec'), may hold values from 64 to 256, as said below
- term_shift: int32 [176], P('op'), may hold values from -1 to 1
- left_env: bfloat16 [176, 64, 256, 256], P('op', 'sec'), may hold values from -0.02734375 to 0.02734375
- right_env: bfloat16 [176, 64, 256, 256], P('op', 'sec'), may hold values from -0.375 to 0.375
Outputs:
- sigma_blocks: bfloat16 [64, 256, 256], P('sec')
The draws below stay inside these ranges and needn't reach their ends.
Inputs may be any that keep to these rules, and one draw needn't show every extreme that they name: `sector_dims`: every sector dimension is a multiple of 64.
All inputs are finite; a program needn't handle non-finite values.
Results may differ from the reference program's by a relative error of at most 0.0051.
Values may be sent and summed in bfloat16 or wider, within the bound.
A program may use at most 64 MiB of HBM per device.

```python
import jax
import jax.numpy as jnp
from jax import lax

B = 256
GRAIN = 64
SECTORS = 64
KTERMS = 176


def draw_sector_dims(key, part):
    key = jax.random.fold_in(key, 7)
    levels = jax.random.randint(key, (SECTORS, 2), 1, B // GRAIN + 1).astype(jnp.int32)
    values = levels * GRAIN
    values = values.at[0, 0].set(B).at[0, 1].set(GRAIN)
    return values.astype(jnp.int32)


def plant(result, own_key, low, largest):
    longest = result.shape.index(max(result.shape))
    spots = []
    for shift in (0, 1):
        where = [jax.random.randint(jax.random.fold_in(own_key, axis), (), 0, length) for axis, length in enumerate(result.shape)]
        where[longest] = (where[longest] + shift) % result.shape[longest]
        spots.append(tuple(where))
    return result.at[spots[0]].set(low).at[spots[1]].set(largest)


def block_levels(rng, extent, cuts, low, top_value):
    gain = 1.0
    for axis_at, parts in cuts:
        draws = jax.random.uniform(jax.random.fold_in(jax.random.fold_in(rng, 6), axis_at), (parts,), jnp.float32, low / len(cuts), top_value / len(cuts))
        gain = gain * jnp.repeat(jnp.exp(draws), extent[axis_at] // parts).reshape((-1,) + (1,) * (len(extent) - 1 - axis_at))
    return gain


def gaussian(stream_key, extent, deviation, limit, shards=(), kind=jnp.bfloat16):
    drawn = deviation * jax.random.normal(stream_key, extent, jnp.float32)
    if shards:
        drawn = drawn * block_levels(stream_key, extent, shards, -0.22, 0.18)
    return jnp.clip(drawn, -limit, limit).astype(kind)


def setup_inputs(seed: int = 0) -> dict:
    key_list = jax.random.split(jax.random.key(seed), 6)
    return {
        "wavefunction": gaussian(key_list[0], (SECTORS, B, B), 1.0, 6.0, ((0, 16),)),
        "sector_dims": draw_sector_dims(jax.random.fold_in(key_list[5], 71), 0),
        "term_shift": plant(jax.random.randint(key_list[2], (KTERMS,), -1, 2), jax.random.fold_in(key_list[2], 1), -1, 1).astype(jnp.int32),
        "left_env": gaussian(key_list[3], (KTERMS, SECTORS, B, B), (B * KTERMS) ** -0.5, 0.02734375, ((0, 16), (1, 16))),
        "right_env": gaussian(key_list[4], (KTERMS, SECTORS, B, B), B ** -0.5, 0.375, ((0, 16), (1, 16))),
    }


def sector_mask(sector_dims, order):
    positions = jnp.arange(order, dtype=jnp.int32)
    rows_ok = positions[None, :] < sector_dims[:, 0:1]
    cols_ok = positions[None, :] < sector_dims[:, 1:2]
    return rows_ok[:, :, None] & cols_ok[:, None, :]


def reference(wavefunction, sector_dims, term_shift, left_env, right_env):
    keep = sector_mask(sector_dims, B)
    masked = jnp.where(keep, wavefunction, jnp.zeros_like(wavefunction))
    blank = jnp.zeros((1, B, B), wavefunction.dtype)
    padded = jnp.concatenate([blank, masked, blank], 0)
    base = jnp.arange(SECTORS, dtype=jnp.int32)

    def one_term(total, pieces):
        shift, left_block, right_block = pieces
        picks = (base + shift + 1).astype(jnp.int32)
        source = jnp.take(padded, picks, axis=0)
        first = jnp.einsum("sab,sbc->sac", left_block.astype(jnp.float32), source.astype(jnp.float32),
                           precision=lax.Precision.HIGHEST).astype(jnp.bfloat16)
        first = lax.optimization_barrier(first)
        second = jnp.einsum("sac,sdc->sad", first.astype(jnp.float32), right_block.astype(jnp.float32),
                            precision=lax.Precision.HIGHEST)
        return total + second, None

    start_total = jnp.zeros((SECTORS, B, B), jnp.float32)
    total, unused = lax.scan(one_term, start_total, (term_shift, left_env, right_env))
    return jnp.where(keep, total, jnp.zeros_like(total)).astype(jnp.bfloat16)
```

```python
import functools

import jax
import jax.numpy as jnp
from jax import lax
from jax.experimental import pallas as pl
from jax.experimental.pallas import tpu as pltpu
from jax.sharding import PartitionSpec as P

MESH = pl.DeviceIdType.MESH
NT = (((1,), (1,)), ((), ()))


def kernel(
    nsec,
    nz,
    dims_ref,
    shift_ref,
    wave_ref,
    left_ref,
    right_ref,
    out_ref,
    wide,
    near,
    left,
    right,
    part,
    sib,
    packed,
    landed,
    wave_sem,
    left_sem,
    right_sem,
    halo_send,
    halo_recv,
    sib_send,
    sib_recv,
    rs_send,
    rs_recv,
    ag_send,
    ag_recv,
    fin_send,
    fin_recv,
):
    order = wide.shape[1]
    terms = left.shape[1]
    rows = order // nz
    sec = lax.axis_index("sec")
    me = lax.axis_index("op")
    z = lax.div(me, 2)
    c = lax.rem(me, 2)

    def peer(d):
        return {"op": lax.rem(z + d, nz) * 2 + c}

    sibling = {"op": z * 2 + 1 - c}

    def beside(d):
        return {"sec": lax.rem(sec + d + nsec, nsec)}

    def sector_of(p, e):
        return 1 - p + e * (1 + 2 * p)

    def load(it):
        s = sector_of(it // 2, c if it % 2 else 1 - c)
        return (
            pltpu.make_async_copy(left_ref.at[:, s], left.at[it], left_sem.at[it]),
            pltpu.make_async_copy(right_ref.at[:, s], right.at[it], right_sem.at[it]),
        )

    def load_wave(s):
        return pltpu.make_async_copy(wave_ref.at[s], wide.at[s + 1], wave_sem.at[s])

    for s in (0, 3, 1, 2):
        load_wave(s).start()
    for it in range(4):
        for copy in load(it):
            copy.start()

    barrier = pltpu.get_barrier_semaphore()
    for d in range(1, nz):
        pl.semaphore_signal(barrier, inc=1, device_id=peer(d), device_id_type=MESH)
    pl.semaphore_signal(barrier, inc=1, device_id=sibling, device_id_type=MESH)
    for d in (-1, 1):
        pl.semaphore_signal(barrier, inc=1, device_id=beside(d), device_id_type=MESH)

    def mask(s):
        row = lax.broadcasted_iota(jnp.int32, (order, order), 0)
        col = lax.broadcasted_iota(jnp.int32, (order, order), 1)
        keep = (row < dims_ref[s, 0]) & (col < dims_ref[s, 1])
        block = wide[s + 1].astype(jnp.float32)
        wide[s + 1] = jnp.where(keep, block, 0.0).astype(jnp.bfloat16)

    for s in (0, 3):
        load_wave(s).wait()
        mask(s)
    pl.semaphore_wait(barrier, nz + 2)

    def halo(i):
        e = c if i == 0 else 1 - c
        return pltpu.make_async_remote_copy(
            src_ref=wide.at[1 + 3 * e],
            dst_ref=wide.at[5 - 5 * e],
            send_sem=halo_send.at[i],
            recv_sem=halo_recv.at[i],
            device_id=beside(2 * e - 1),
            device_id_type=MESH,
        )

    for i in range(2):
        halo(i).start()
    for s in (1, 2):
        load_wave(s).wait()
        mask(s)

    def to_sibling(p):
        return pltpu.make_async_remote_copy(
            src_ref=part.at[2 * p],
            dst_ref=sib.at[p],
            send_sem=sib_send.at[p],
            recv_sem=sib_recv.at[p],
            device_id=sibling,
            device_id_type=MESH,
        )

    def scatter(p, d):
        chunk = lax.rem(z + d, nz) * rows
        return pltpu.make_async_remote_copy(
            src_ref=packed.at[p, pl.ds(pl.multiple_of(chunk, rows), rows)],
            dst_ref=landed.at[p, d - 1],
            send_sem=rs_send.at[p, d - 1],
            recv_sem=rs_recv.at[p, d - 1],
            device_id=peer(d),
            device_id_type=MESH,
        )

    mine = pl.ds(pl.multiple_of(z * rows, rows), rows)

    def gather(p, d):
        own = sector_of(p, c)
        return pltpu.make_async_remote_copy(
            src_ref=out_ref.at[own, mine],
            dst_ref=out_ref.at[own, mine],
            send_sem=ag_send.at[p, d - 1],
            recv_sem=ag_recv.at[p, d - 1],
            device_id=peer(d),
            device_id_type=MESH,
        )

    def final(p):
        own = sector_of(p, c)
        return pltpu.make_async_remote_copy(
            src_ref=out_ref.at[own],
            dst_ref=out_ref.at[own],
            send_sem=fin_send.at[p],
            recv_sem=fin_recv.at[p],
            device_id=sibling,
            device_id_type=MESH,
        )

    far = sorted(range(1, nz), key=lambda d: -min(d, nz - d))

    def step(it, carry):
        p = lax.div(it, 2)
        q = lax.rem(it, 2)
        e = q * c + (1 - q) * (1 - c)
        s = sector_of(p, e)
        for i in range(2):

            @pl.when(it == 2 + i)
            def _():
                halo(i).wait_recv()
                f = c if i == 0 else 1 - c

                @pl.when(sec == (nsec - 1) * (1 - f))
                def _():
                    wide[5 - 5 * f] = jnp.zeros((order, order), jnp.bfloat16)

        for n in range(3):
            near[n] = wide[s + n]
        pltpu.make_async_copy(left_ref.at[:, s], left.at[it], left_sem.at[it]).wait()
        pltpu.make_async_copy(right_ref.at[:, s], right.at[it], right_sem.at[it]).wait()
        total = None
        for k in range(terms):
            first = jnp.dot(
                left[it, k], near[shift_ref[k] + 1], preferred_element_type=jnp.float32
            ).astype(jnp.bfloat16)
            term = lax.dot_general(first, right[it, k], NT, preferred_element_type=jnp.float32)
            total = term if total is None else total + term
        part[it] = total
        for p_now in range(2):

            @pl.when(it == 2 * p_now)
            def _():
                to_sibling(p_now).start()

            @pl.when(it == 2 * p_now + 1)
            def _():
                to_sibling(p_now).wait_recv()
                packed[p_now] = (part[2 * p_now + 1] + sib[p_now]).astype(jnp.bfloat16)
                for d in far:
                    scatter(p_now, d).start()

        return carry

    lax.fori_loop(0, 4, step, 0)

    for p in range(2):
        total = part[2 * p + 1, mine] + sib[p, mine]
        for d in range(1, nz):
            scatter(p, d).wait_recv()
            total += landed[p, d - 1].astype(jnp.float32)
        out_ref[sector_of(p, c), mine] = total.astype(jnp.bfloat16)
        for d in far:
            gather(p, d).start()
    for p in range(2):
        for d in range(1, nz):
            gather(p, d).wait_recv()
        final(p).start()
    for i in range(2):
        halo(i).wait_send()
        to_sibling(i).wait_send()
        for d in range(1, nz):
            scatter(i, d).wait_send()
            gather(i, d).wait_send()
    for p in range(2):
        final(p).wait()


def body(nsec, nz, wavefunction, sector_dims, term_shift, left_env, right_env):
    count, order, _ = wavefunction.shape
    terms = left_env.shape[0]
    rows = order // nz
    bf16, f32 = jnp.bfloat16, jnp.float32
    dma = pltpu.SemaphoreType.DMA
    smem = pl.BlockSpec(memory_space=pltpu.SMEM)
    anywhere = pl.BlockSpec(memory_space=pl.ANY)
    total = pl.pallas_call(
        functools.partial(kernel, nsec, nz),
        out_shape=pltpu.VMEM((count, order, order), bf16),
        in_specs=[smem, smem, anywhere, anywhere, anywhere],
        out_specs=pl.BlockSpec(memory_space=pltpu.VMEM),
        scratch_shapes=[
            pltpu.VMEM((count + 2, order, order), bf16),
            pltpu.VMEM((3, order, order), bf16),
            pltpu.VMEM((count, terms, order, order), bf16),
            pltpu.VMEM((count, terms, order, order), bf16),
            pltpu.VMEM((count, order, order), f32),
            pltpu.VMEM((2, order, order), f32),
            pltpu.VMEM((2, order, order), bf16),
            pltpu.VMEM((2, nz - 1, rows, order), bf16),
            dma((count,)),
            dma((count,)),
            dma((count,)),
            dma((2,)),
            dma((2,)),
            dma((2,)),
            dma((2,)),
            dma((2, nz - 1)),
            dma((2, nz - 1)),
            dma((2, nz - 1)),
            dma((2, nz - 1)),
            dma((2,)),
            dma((2,)),
        ],
        compiler_params=pltpu.CompilerParams(
            collective_id=0, has_side_effects=True, vmem_limit_bytes=32 << 20
        ),
    )(sector_dims, term_shift, wavefunction, left_env, right_env)
    positions = jnp.arange(order, dtype=jnp.int32)
    rows_ok = positions[None, :] < sector_dims[:, 0:1]
    cols_ok = positions[None, :] < sector_dims[:, 1:2]
    keep = rows_ok[:, :, None] & cols_ok[:, None, :]
    return jnp.where(keep, total, jnp.zeros_like(total))


def solution(mesh):
    nsec, nop = mesh.shape["sec"], mesh.shape["op"]
    return jax.shard_map(
        functools.partial(body, nsec, nop // 2),
        mesh=mesh,
        in_specs=(
            P("sec", None, None),
            P("sec", None),
            P("op"),
            P("op", "sec", None, None),
            P("op", "sec", None, None),
        ),
        out_specs=P("sec", None, None),
        check_vma=False,
    )
```

```python
import functools

import jax
import jax.numpy as jnp
from jax import lax
from jax.experimental import pallas as pl
from jax.experimental.pallas import tpu as pltpu
from jax.sharding import PartitionSpec as P

MESH = pl.DeviceIdType.MESH
NT = (((1,), (1,)), ((), ()))


def kernel(
    nsec,
    nz,
    dims_hbm,
    shift_hbm,
    wave_ref,
    left_ref,
    right_ref,
    out_ref,
    wide,
    near,
    left,
    right,
    part,
    sib,
    packed,
    landed,
    dims_ref,
    shift_ref,
    small_sem,
    wave_sem,
    left_sem,
    right_sem,
    halo_send,
    halo_recv,
    sib_send,
    sib_recv,
    rs_send,
    rs_recv,
    ag_send,
    ag_recv,
    fin_send,
    fin_recv,
):
    order = wide.shape[1]
    terms = left.shape[1]
    rows = order // nz
    sec = lax.axis_index("sec")
    me = lax.axis_index("op")
    z = lax.div(me, 2)
    c = lax.rem(me, 2)

    def peer(d):
        return {"op": lax.rem(z + d, nz) * 2 + c}

    sibling = {"op": z * 2 + 1 - c}

    def beside(d):
        return {"sec": lax.rem(sec + d + nsec, nsec)}

    def sector_of(p, e):
        return 1 - p + e * (1 + 2 * p)

    def load(it):
        s = sector_of(it // 2, c if it % 2 else 1 - c)
        return (
            pltpu.make_async_copy(left_ref.at[:, s], left.at[it], left_sem.at[it]),
            pltpu.make_async_copy(right_ref.at[:, s], right.at[it], right_sem.at[it]),
        )

    def load_wave(s):
        return pltpu.make_async_copy(wave_ref.at[s], wide.at[s + 1], wave_sem.at[s])

    load_dims = pltpu.make_async_copy(dims_hbm, dims_ref, small_sem.at[0])
    load_shift = pltpu.make_async_copy(shift_hbm, shift_ref, small_sem.at[1])
    load_dims.start()
    for s in (0, 3, 1, 2):
        load_wave(s).start()
    load_shift.start()
    for it in range(4):
        for copy in load(it):
            copy.start()

    barrier = pltpu.get_barrier_semaphore()
    for d in range(1, nz):
        pl.semaphore_signal(barrier, inc=1, device_id=peer(d), device_id_type=MESH)
    pl.semaphore_signal(barrier, inc=1, device_id=sibling, device_id_type=MESH)
    for d in (-1, 1):
        pl.semaphore_signal(barrier, inc=1, device_id=beside(d), device_id_type=MESH)

    def masked(block, s, start):
        row = lax.broadcasted_iota(jnp.int32, block.shape, 0) + start
        col = lax.broadcasted_iota(jnp.int32, block.shape, 1)
        keep = (row < dims_ref[0, s]) & (col < dims_ref[1, s])
        return jnp.where(keep, block, 0.0).astype(jnp.bfloat16)

    def mask(s):
        wide[s + 1] = masked(wide[s + 1].astype(jnp.float32), s, 0)

    load_dims.wait()
    for s in (0, 3):
        load_wave(s).wait()
        mask(s)
    pl.semaphore_wait(barrier, nz + 2)

    def halo(i):
        e = c if i == 0 else 1 - c
        return pltpu.make_async_remote_copy(
            src_ref=wide.at[1 + 3 * e],
            dst_ref=wide.at[5 - 5 * e],
            send_sem=halo_send.at[i],
            recv_sem=halo_recv.at[i],
            device_id=beside(2 * e - 1),
            device_id_type=MESH,
        )

    for i in range(2):
        halo(i).start()
    for s in (1, 2):
        load_wave(s).wait()
        mask(s)

    load_shift.wait()

    def to_sibling(p):
        return pltpu.make_async_remote_copy(
            src_ref=part.at[2 * p],
            dst_ref=sib.at[p],
            send_sem=sib_send.at[p],
            recv_sem=sib_recv.at[p],
            device_id=sibling,
            device_id_type=MESH,
        )

    def scatter(p, d):
        chunk = lax.rem(z + d, nz) * rows
        return pltpu.make_async_remote_copy(
            src_ref=packed.at[p, pl.ds(pl.multiple_of(chunk, rows), rows)],
            dst_ref=landed.at[p, d - 1],
            send_sem=rs_send.at[p, d - 1],
            recv_sem=rs_recv.at[p, d - 1],
            device_id=peer(d),
            device_id_type=MESH,
        )

    mine = pl.ds(pl.multiple_of(z * rows, rows), rows)

    def gather(p, d):
        own = sector_of(p, c)
        return pltpu.make_async_remote_copy(
            src_ref=out_ref.at[own, mine],
            dst_ref=out_ref.at[own, mine],
            send_sem=ag_send.at[p, d - 1],
            recv_sem=ag_recv.at[p, d - 1],
            device_id=peer(d),
            device_id_type=MESH,
        )

    def final(p):
        own = sector_of(p, c)
        return pltpu.make_async_remote_copy(
            src_ref=out_ref.at[own],
            dst_ref=out_ref.at[own],
            send_sem=fin_send.at[p],
            recv_sem=fin_recv.at[p],
            device_id=sibling,
            device_id_type=MESH,
        )

    far = sorted(range(1, nz), key=lambda d: -min(d, nz - d))

    def step(it, carry):
        p = lax.div(it, 2)
        q = lax.rem(it, 2)
        e = q * c + (1 - q) * (1 - c)
        s = sector_of(p, e)
        for i in range(2):

            @pl.when(it == 2 + i)
            def _():
                halo(i).wait_recv()
                f = c if i == 0 else 1 - c

                @pl.when(sec == (nsec - 1) * (1 - f))
                def _():
                    wide[5 - 5 * f] = jnp.zeros((order, order), jnp.bfloat16)

        for n in range(3):
            near[n] = wide[s + n]
        pltpu.make_async_copy(left_ref.at[:, s], left.at[it], left_sem.at[it]).wait()
        pltpu.make_async_copy(right_ref.at[:, s], right.at[it], right_sem.at[it]).wait()
        total = None
        for k in range(terms):
            first = jnp.dot(
                left[it, k], near[shift_ref[k] + 1], preferred_element_type=jnp.float32
            ).astype(jnp.bfloat16)
            term = lax.dot_general(first, right[it, k], NT, preferred_element_type=jnp.float32)
            total = term if total is None else total + term
        part[it] = total
        for p_now in range(2):

            @pl.when(it == 2 * p_now)
            def _():
                to_sibling(p_now).start()

            @pl.when(it == 2 * p_now + 1)
            def _():
                to_sibling(p_now).wait_recv()
                packed[p_now] = (part[2 * p_now + 1] + sib[p_now]).astype(jnp.bfloat16)
                for d in far:
                    scatter(p_now, d).start()

        return carry

    lax.fori_loop(0, 4, step, 0)

    for p in range(2):
        total = part[2 * p + 1, mine] + sib[p, mine]
        for d in range(1, nz):
            scatter(p, d).wait_recv()
            total += landed[p, d - 1].astype(jnp.float32)
        own = sector_of(p, c)
        out_ref[own, mine] = masked(total, own, z * rows)
        for d in far:
            gather(p, d).start()
    for p in range(2):
        for d in range(1, nz):
            gather(p, d).wait_recv()
        final(p).start()
    for i in range(2):
        halo(i).wait_send()
        to_sibling(i).wait_send()
        for d in range(1, nz):
            scatter(i, d).wait_send()
            gather(i, d).wait_send()
    for p in range(2):
        final(p).wait()


def body(nsec, nz, wavefunction, sector_dims, term_shift, left_env, right_env):
    count, order, _ = wavefunction.shape
    terms = left_env.shape[0]
    rows = order // nz
    bf16, f32 = jnp.bfloat16, jnp.float32
    dma = pltpu.SemaphoreType.DMA
    hbm = pl.BlockSpec(memory_space=pltpu.HBM)
    return pl.pallas_call(
        functools.partial(kernel, nsec, nz),
        out_shape=pltpu.VMEM((count, order, order), bf16),
        in_specs=[hbm] * 5,
        out_specs=pl.BlockSpec(memory_space=pltpu.VMEM),
        scratch_shapes=[
            pltpu.VMEM((count + 2, order, order), bf16),
            pltpu.VMEM((3, order, order), bf16),
            pltpu.VMEM((count, terms, order, order), bf16),
            pltpu.VMEM((count, terms, order, order), bf16),
            pltpu.VMEM((count, order, order), f32),
            pltpu.VMEM((2, order, order), f32),
            pltpu.VMEM((2, order, order), bf16),
            pltpu.VMEM((2, nz - 1, rows, order), bf16),
            pltpu.SMEM((2, count), jnp.int32),
            pltpu.SMEM((terms,), jnp.int32),
            dma((2,)),
            dma((count,)),
            dma((count,)),
            dma((count,)),
            dma((2,)),
            dma((2,)),
            dma((2,)),
            dma((2,)),
            dma((2, nz - 1)),
            dma((2, nz - 1)),
            dma((2, nz - 1)),
            dma((2, nz - 1)),
            dma((2,)),
            dma((2,)),
        ],
        compiler_params=pltpu.CompilerParams(
            collective_id=0, has_side_effects=True, vmem_limit_bytes=32 << 20
        ),
    )(*(
        pltpu.with_memory_space_constraint(x, pltpu.HBM)
        for x in (sector_dims.T, term_shift, wavefunction, left_env, right_env)
    ))


def solution(mesh):
    nsec, nop = mesh.shape["sec"], mesh.shape["op"]
    return jax.shard_map(
        functools.partial(body, nsec, nop // 2),
        mesh=mesh,
        in_specs=(
            P("sec", None, None),
            P("sec", None),
            P("op"),
            P("op", "sec", None, None),
            P("op", "sec", None, None),
        ),
        out_specs=P("sec", None, None),
        check_vma=False,
    )
```

```python
import functools

import jax
import jax.numpy as jnp
from jax import lax
from jax.experimental import pallas as pl
from jax.experimental.pallas import tpu as pltpu
from jax.sharding import PartitionSpec as P

MESH = pl.DeviceIdType.MESH
NT = (((1,), (1,)), ((), ()))


def kernel(
    nsec,
    nz,
    dims_hbm,
    shift_hbm,
    wave_ref,
    left_ref,
    right_ref,
    out_ref,
    wide,
    near,
    left,
    right,
    part,
    sib,
    packed,
    landed,
    dims_ref,
    shift_ref,
    small_sem,
    wave_sem,
    left_sem,
    right_sem,
    halo_send,
    halo_recv,
    sib_send,
    sib_recv,
    rs_send,
    rs_recv,
    ag_send,
    ag_recv,
    fin_send,
    fin_recv,
    ready,
):
    order = wide.shape[1]
    terms = left.shape[1]
    rows = order // nz
    sec = lax.axis_index("sec")
    me = lax.axis_index("op")
    z = lax.div(me, 2)
    c = lax.rem(me, 2)

    def peer(d):
        return {"op": lax.rem(z + d, nz) * 2 + c}

    sibling = {"op": z * 2 + 1 - c}
    near_z = (1, 2, nz - 2, nz - 1)

    def beside(d):
        return {"sec": lax.rem(sec + d + nsec, nsec)}

    def sector_of(p, e):
        return 1 - p + e * (1 + 2 * p)

    def load(it):
        q = lax.rem(it, 2)
        s = sector_of(lax.div(it, 2), q * c + (1 - q) * (1 - c))
        return (
            pltpu.make_async_copy(left_ref.at[:, s], left.at[it], left_sem.at[it]),
            pltpu.make_async_copy(right_ref.at[:, s], right.at[it], right_sem.at[it]),
        )

    def load_wave(s):
        return pltpu.make_async_copy(wave_ref.at[s], wide.at[s + 1], wave_sem.at[s])

    load_dims = pltpu.make_async_copy(dims_hbm, dims_ref, small_sem.at[0])
    load_shift = pltpu.make_async_copy(shift_hbm, shift_ref, small_sem.at[1])
    load_dims.start()
    waves = (3 * c, 3 - 3 * c, 1, 2)
    for s in waves:
        load_wave(s).start()
    load_shift.start()
    for copy in load(0):
        copy.start()

    barrier = pltpu.get_barrier_semaphore()
    greeted = [beside(-1), beside(1), sibling] + [peer(d) for d in near_z]
    for device in greeted:
        pl.semaphore_signal(barrier, inc=1, device_id=device, device_id_type=MESH)

    def masked(block, s, start):
        row = lax.broadcasted_iota(jnp.int32, block.shape, 0) + start
        col = lax.broadcasted_iota(jnp.int32, block.shape, 1)
        keep = (row < dims_ref[0, s]) & (col < dims_ref[1, s])
        return jnp.where(keep, block, 0.0).astype(jnp.bfloat16)

    def mask(s):
        wide[s + 1] = masked(wide[s + 1].astype(jnp.float32), s, 0)

    load_dims.wait()
    load_wave(waves[0]).wait()
    mask(waves[0])
    pl.semaphore_wait(barrier, len(greeted))

    halo = pltpu.make_async_remote_copy(
        src_ref=wide.at[1 + 3 * c],
        dst_ref=wide.at[5 - 5 * c],
        send_sem=halo_send.at[0],
        recv_sem=halo_recv.at[0],
        device_id=beside(2 * c - 1),
        device_id_type=MESH,
    )
    halo.start()
    for d in (2, nz - 2):
        pl.semaphore_signal(ready, inc=1, device_id=peer(d), device_id_type=MESH)

    def passed(slot):
        return pltpu.make_async_remote_copy(
            src_ref=wide.at[slot],
            dst_ref=wide.at[slot],
            send_sem=halo_send.at[1],
            recv_sem=halo_recv.at[1],
            device_id=sibling,
            device_id_type=MESH,
        )

    for s in waves[1:]:
        load_wave(s).wait()
        mask(s)
    load_shift.wait()

    def to_sibling(p):
        return pltpu.make_async_remote_copy(
            src_ref=part.at[2 * p],
            dst_ref=sib.at[p],
            send_sem=sib_send.at[p],
            recv_sem=sib_recv.at[p],
            device_id=sibling,
            device_id_type=MESH,
        )

    def scatter(p, d):
        chunk = lax.rem(z + d, nz) * rows
        return pltpu.make_async_remote_copy(
            src_ref=packed.at[p, pl.ds(pl.multiple_of(chunk, rows), rows)],
            dst_ref=landed.at[p, d - 1],
            send_sem=rs_send.at[p, d - 1],
            recv_sem=rs_recv.at[p, d - 1],
            device_id=peer(d),
            device_id_type=MESH,
        )

    mine = pl.ds(pl.multiple_of(z * rows, rows), rows)

    def gather(p, d):
        own = sector_of(p, c)
        return pltpu.make_async_remote_copy(
            src_ref=out_ref.at[own, mine],
            dst_ref=out_ref.at[own, mine],
            send_sem=ag_send.at[p, d - 1],
            recv_sem=ag_recv.at[p, d - 1],
            device_id=peer(d),
            device_id_type=MESH,
        )

    def final(p):
        own = sector_of(p, c)
        return pltpu.make_async_remote_copy(
            src_ref=out_ref.at[own],
            dst_ref=out_ref.at[own],
            send_sem=fin_send.at[p],
            recv_sem=fin_recv.at[p],
            device_id=sibling,
            device_id_type=MESH,
        )

    far = sorted(range(1, nz), key=lambda d: -min(d, nz - d))

    def step(it, carry):
        p = lax.div(it, 2)
        q = lax.rem(it, 2)
        e = q * c + (1 - q) * (1 - c)
        s = sector_of(p, e)

        @pl.when(it == 2)
        def _():
            halo.wait_recv()

            @pl.when(sec == (nsec - 1) * (1 - c))
            def _():
                wide[5 - 5 * c] = jnp.zeros((order, order), jnp.bfloat16)

            passed(5 - 5 * c).start()

        @pl.when(it == 3)
        def _():
            passed(5 * c).wait_recv()

        for n in range(3):
            near[n] = wide[s + n]
        left_now, right_now = load(it)

        @pl.when(it == 0)
        def _():
            for later in range(1, 4):
                for copy in load(later):
                    copy.start()

        left_now.wait()
        right_now.wait()

        def first(k):
            return jnp.dot(
                left[it, k], near[shift_ref[k] + 1], preferred_element_type=jnp.float32
            ).astype(jnp.bfloat16)

        total, ahead = None, first(0)
        for k in range(terms):
            now, ahead = ahead, first(k + 1) if k + 1 < terms else None
            term = lax.dot_general(now, right[it, k], NT, preferred_element_type=jnp.float32)
            total = term if total is None else total + term
        part[it] = total

        @pl.when(q == 0)
        def _():
            to_sibling(p).start()

        @pl.when(q == 1)
        def _():
            to_sibling(p).wait_recv()
            packed[p] = (total + sib[p]).astype(jnp.bfloat16)

            @pl.when(p == 0)
            def _():
                pl.semaphore_wait(ready, 2)

            for d in far:
                scatter(p, d).start()

        return carry

    lax.fori_loop(0, 4, step, 0)

    def reduce(p, carry):
        total = part[2 * p + 1, mine] + sib[p, mine]
        for d in range(1, nz):
            scatter(p, d).wait_recv()
            total += landed[p, d - 1].astype(jnp.float32)
        own = sector_of(p, c)
        out_ref[own, mine] = masked(total, own, z * rows)
        for d in far:
            gather(p, d).start()
        return carry

    def spread(p, carry):
        for d in range(1, nz):
            gather(p, d).wait_recv()
        final(p).start()
        return carry

    def finish(p, carry):
        to_sibling(p).wait_send()
        for d in range(1, nz):
            scatter(p, d).wait_send()
            gather(p, d).wait_send()
        final(p).wait()
        return carry

    lax.fori_loop(0, 2, reduce, 0)
    lax.fori_loop(0, 2, spread, 0)
    lax.fori_loop(0, 2, finish, 0)
    halo.wait_send()
    passed(5 - 5 * c).wait_send()


def body(nsec, nz, wavefunction, sector_dims, term_shift, left_env, right_env):
    count, order, _ = wavefunction.shape
    terms = left_env.shape[0]
    rows = order // nz
    bf16, f32 = jnp.bfloat16, jnp.float32
    dma = pltpu.SemaphoreType.DMA
    hbm = pl.BlockSpec(memory_space=pltpu.HBM)
    return pl.pallas_call(
        functools.partial(kernel, nsec, nz),
        out_shape=pltpu.VMEM((count, order, order), bf16),
        in_specs=[hbm] * 5,
        out_specs=pl.BlockSpec(memory_space=pltpu.VMEM),
        scratch_shapes=[
            pltpu.VMEM((count + 2, order, order), bf16),
            pltpu.VMEM((3, order, order), bf16),
            pltpu.VMEM((count, terms, order, order), bf16),
            pltpu.VMEM((count, terms, order, order), bf16),
            pltpu.VMEM((count, order, order), f32),
            pltpu.VMEM((2, order, order), f32),
            pltpu.VMEM((2, order, order), bf16),
            pltpu.VMEM((2, nz - 1, rows, order), bf16),
            pltpu.SMEM((2, count), jnp.int32),
            pltpu.SMEM((terms,), jnp.int32),
            dma((2,)),
            dma((count,)),
            dma((count,)),
            dma((count,)),
            dma((2,)),
            dma((2,)),
            dma((2,)),
            dma((2,)),
            dma((2, nz - 1)),
            dma((2, nz - 1)),
            dma((2, nz - 1)),
            dma((2, nz - 1)),
            dma((2,)),
            dma((2,)),
            pltpu.SemaphoreType.REGULAR,
        ],
        compiler_params=pltpu.CompilerParams(
            collective_id=0, has_side_effects=True, vmem_limit_bytes=32 << 20
        ),
    )(*(
        pltpu.with_memory_space_constraint(x, pltpu.HBM)
        for x in (sector_dims.T, term_shift, wavefunction, left_env, right_env)
    ))


def solution(mesh):
    nsec, nop = mesh.shape["sec"], mesh.shape["op"]
    return jax.shard_map(
        functools.partial(body, nsec, nop // 2),
        mesh=mesh,
        in_specs=(
            P("sec", None, None),
            P("sec", None),
            P("op"),
            P("op", "sec", None, None),
            P("op", "sec", None, None),
        ),
        out_specs=P("sec", None, None),
        check_vma=False,
    )
```

```python
import functools

import jax
import jax.numpy as jnp
from jax import lax
from jax.experimental import pallas as pl
from jax.experimental.pallas import tpu as pltpu
from jax.sharding import PartitionSpec as P

MESH = pl.DeviceIdType.MESH
NT = (((1,), (1,)), ((), ()))


def kernel(
    nsec,
    nz,
    dims_hbm,
    shift_hbm,
    wave_ref,
    left_ref,
    right_ref,
    out_ref,
    wide,
    near,
    left,
    right,
    part,
    sib,
    packed,
    landed,
    done,
    dims_ref,
    shift_ref,
    small_sem,
    wave_sem,
    left_sem,
    right_sem,
    halo_send,
    halo_recv,
    sib_send,
    sib_recv,
    rs_send,
    rs_recv,
    ag_send,
    ag_recv,
    share_send,
    share_recv,
    ready,
):
    order = wide.shape[1]
    terms = left.shape[1]
    rows = order // nz
    sec = lax.axis_index("sec")
    me = lax.axis_index("op")
    z = lax.div(me, 2)
    c = lax.rem(me, 2)

    def peer(d):
        return {"op": lax.rem(z + d, nz) * 2 + 1}

    sibling = {"op": z * 2 + 1 - c}
    near_z = (1, 2, nz - 2, nz - 1)

    def beside(d, core):
        return {"sec": lax.rem(sec + d + nsec, nsec), "op": z * 2 + core}

    def sector_of(p, e):
        return 1 - p + e * (1 + 2 * p)

    def load(it):
        q = lax.rem(it, 2)
        s = sector_of(lax.div(it, 2), q * c + (1 - q) * (1 - c))
        return (
            pltpu.make_async_copy(left_ref.at[:, s], left.at[it], left_sem.at[it]),
            pltpu.make_async_copy(right_ref.at[:, s], right.at[it], right_sem.at[it]),
        )

    def load_wave(s):
        return pltpu.make_async_copy(wave_ref.at[s], wide.at[s + 1], wave_sem.at[s])

    load_dims = pltpu.make_async_copy(dims_hbm, dims_ref, small_sem.at[0])
    load_shift = pltpu.make_async_copy(shift_hbm, shift_ref, small_sem.at[1])
    load_dims.start()
    for s in (3, 0, 1, 2):
        load_wave(s).start()
    load_shift.start()
    for copy in load(0):
        copy.start()

    barrier = pltpu.get_barrier_semaphore()

    def signal(sem, device):
        pl.semaphore_signal(sem, inc=1, device_id=device, device_id_type=MESH)

    signal(barrier, sibling)

    @pl.when(c == 1)
    def _():
        signal(barrier, beside(-1, 1))
        for d in near_z:
            signal(barrier, peer(d))
            signal(barrier, {"op": lax.rem(z + d, nz) * 2})

    @pl.when(c == 0)
    def _():
        signal(barrier, beside(1, 1))

    def masked(block, s, start):
        row = lax.broadcasted_iota(jnp.int32, block.shape, 0) + start
        col = lax.broadcasted_iota(jnp.int32, block.shape, 1)
        keep = (row < dims_ref[0, s]) & (col < dims_ref[1, s])
        return jnp.where(keep, block, 0.0).astype(jnp.bfloat16)

    def mask(s):
        wide[s + 1] = masked(wide[s + 1].astype(jnp.float32), s, 0)

    load_dims.wait()
    for s in (3, 0):
        load_wave(s).wait()
        mask(s)
    pl.semaphore_wait(barrier, 5 + 2 * c)

    def halo(i):
        return pltpu.make_async_remote_copy(
            src_ref=wide.at[4 - 3 * i],
            dst_ref=wide.at[5 * i],
            send_sem=halo_send.at[i],
            recv_sem=halo_recv.at[0],
            device_id=beside(1 - 2 * i, 1 - i),
            device_id_type=MESH,
        )

    @pl.when(c == 1)
    def _():
        for i in (1, 0):
            halo(i).start()
        for d in (2, nz - 2):
            signal(ready, peer(d))

    def passed(slot):
        return pltpu.make_async_remote_copy(
            src_ref=wide.at[slot],
            dst_ref=wide.at[slot],
            send_sem=halo_send.at[2],
            recv_sem=halo_recv.at[1],
            device_id=sibling,
            device_id_type=MESH,
        )

    for s in (1, 2):
        load_wave(s).wait()
        mask(s)
    load_shift.wait()

    def to_sibling(p):
        return pltpu.make_async_remote_copy(
            src_ref=part.at[2 * p],
            dst_ref=sib.at[p],
            send_sem=sib_send.at[p],
            recv_sem=sib_recv.at[p],
            device_id=sibling,
            device_id_type=MESH,
        )

    def scatter(p, d):
        chunk = lax.rem(z + d, nz) * rows
        return pltpu.make_async_remote_copy(
            src_ref=packed.at[p, pl.ds(pl.multiple_of(chunk, rows), rows)],
            dst_ref=landed.at[p, c * (nz - 1) + d - 1],
            send_sem=rs_send.at[p],
            recv_sem=rs_recv.at[p],
            device_id=peer(d),
            device_id_type=MESH,
        )

    mine = pl.ds(pl.multiple_of(z * rows, rows), rows)

    def hand_over(p):
        return pltpu.make_async_remote_copy(
            src_ref=packed.at[p, mine],
            dst_ref=landed.at[p, 2 * (nz - 1)],
            send_sem=rs_send.at[p],
            recv_sem=rs_recv.at[p],
            device_id=sibling,
            device_id_type=MESH,
        )

    def gather(p, d):
        return pltpu.make_async_remote_copy(
            src_ref=done.at[p, z],
            dst_ref=done.at[p, z],
            send_sem=ag_send.at[p],
            recv_sem=ag_recv.at[p, d - 1],
            device_id=peer(d),
            device_id_type=MESH,
        )

    def share(p, d):
        chunk = lax.rem(z - d + nz, nz)
        return pltpu.make_async_remote_copy(
            src_ref=done.at[p, chunk],
            dst_ref=done.at[p, chunk],
            send_sem=share_send.at[p],
            recv_sem=share_recv.at[p],
            device_id=sibling,
            device_id_type=MESH,
        )

    def wait_all(ref, sem):
        pltpu.make_async_copy(ref, ref, sem).wait()

    far = sorted(range(1, nz), key=lambda d: -min(d, nz - d))

    def step(it, carry):
        p = lax.div(it, 2)
        q = lax.rem(it, 2)
        e = q * c + (1 - q) * (1 - c)
        s = sector_of(p, e)

        @pl.when(it == 2)
        def _():
            halo(1 - c).wait_recv()

            @pl.when(sec == (nsec - 1) * (1 - c))
            def _():
                wide[5 - 5 * c] = jnp.zeros((order, order), jnp.bfloat16)

            passed(5 - 5 * c).start()

        @pl.when(it == 3)
        def _():
            passed(5 * c).wait_recv()

        for n in range(3):
            near[n] = wide[s + n]
        left_now, right_now = load(it)

        @pl.when(it == 0)
        def _():
            for later in range(1, 4):
                for copy in load(later):
                    copy.start()

        left_now.wait()
        right_now.wait()

        def first(k):
            return jnp.dot(
                left[it, k], near[shift_ref[k] + 1], preferred_element_type=jnp.float32
            ).astype(jnp.bfloat16)

        total, ahead = None, first(0)
        for k in range(terms):
            now, ahead = ahead, first(k + 1) if k + 1 < terms else None
            term = lax.dot_general(now, right[it, k], NT, preferred_element_type=jnp.float32)
            total = term if total is None else total + term
        part[it] = total

        @pl.when(q == 0)
        def _():
            to_sibling(p).start()

        @pl.when(q == 1)
        def _():
            to_sibling(p).wait_recv()
            packed[p] = (total + sib[p]).astype(jnp.bfloat16)

            @pl.when(p == 0)
            def _():
                pl.semaphore_wait(ready, 1 + c)

                @pl.when(c == 1)
                def _():
                    signal(ready, sibling)

            for d in far:
                scatter(p, d).start()

            @pl.when(c == 0)
            def _():
                hand_over(p).start()

        return carry

    lax.fori_loop(0, 4, step, 0)

    def reduce(p, carry):
        mine_now = part[2 * p + 1, mine] + sib[p, mine]
        wait_all(landed.at[p], rs_recv.at[p])
        sums = [landed[p, 2 * (nz - 1)].astype(jnp.float32), mine_now]
        for d in range(1, nz):
            for core in range(2):
                sums[core] += landed[p, core * (nz - 1) + d - 1].astype(jnp.float32)
        for core in range(2):
            done[p, z, core] = masked(sums[core], sector_of(p, core), z * rows)
        for d in far:
            gather(p, d).start()
        share(p, 0).start()
        return carry

    def pass_on(p, carry):
        for d in reversed(far):
            gather(p, d).wait_recv()
            share(p, d).start()
        return carry

    def place(p):
        for core in range(2):
            for n in range(nz):
                out_ref[sector_of(p, core), pl.ds(n * rows, rows)] = done[p, n, core]

    @pl.when(c == 1)
    def _():
        lax.fori_loop(0, 2, reduce, 0)
        lax.fori_loop(0, 2, pass_on, 0)

    def finish(p, carry):
        to_sibling(p).wait_send()

        @pl.when(c == 0)
        def _():
            wait_all(packed.at[p], rs_send.at[p])
            wait_all(done.at[p], share_recv.at[p])

        place(p)

        @pl.when(c == 1)
        def _():
            wait_all(landed.at[p, pl.ds(0, nz - 1)], rs_send.at[p])
            wait_all(done.at[p, pl.ds(0, nz - 1)], ag_send.at[p])
            wait_all(done.at[p], share_send.at[p])

        return carry

    passed(5 - 5 * c).wait_send()

    @pl.when(c == 1)
    def _():
        for i in range(2):
            halo(i).wait_send()

    lax.fori_loop(0, 2, finish, 0)


def body(nsec, nz, wavefunction, sector_dims, term_shift, left_env, right_env):
    count, order, _ = wavefunction.shape
    terms = left_env.shape[0]
    rows = order // nz
    bf16, f32 = jnp.bfloat16, jnp.float32
    dma = pltpu.SemaphoreType.DMA
    hbm = pl.BlockSpec(memory_space=pltpu.HBM)
    return pl.pallas_call(
        functools.partial(kernel, nsec, nz),
        out_shape=pltpu.VMEM((count, order, order), bf16),
        in_specs=[hbm] * 5,
        out_specs=pl.BlockSpec(memory_space=pltpu.VMEM),
        scratch_shapes=[
            pltpu.VMEM((count + 2, order, order), bf16),
            pltpu.VMEM((3, order, order), bf16),
            pltpu.VMEM((count, terms, order, order), bf16),
            pltpu.VMEM((count, terms, order, order), bf16),
            pltpu.VMEM((count, order, order), f32),
            pltpu.VMEM((2, order, order), f32),
            pltpu.VMEM((2, order, order), bf16),
            pltpu.VMEM((2, 2 * nz - 1, rows, order), bf16),
            pltpu.VMEM((2, nz, 2, rows, order), bf16),
            pltpu.SMEM((2, count), jnp.int32),
            pltpu.SMEM((terms,), jnp.int32),
            dma((2,)),
            dma((count,)),
            dma((count,)),
            dma((count,)),
            dma((3,)),
            dma((2,)),
            dma((2,)),
            dma((2,)),
            dma((2,)),
            dma((2,)),
            dma((2,)),
            dma((2, nz - 1)),
            dma((2,)),
            dma((2,)),
            pltpu.SemaphoreType.REGULAR,
        ],
        compiler_params=pltpu.CompilerParams(
            collective_id=0, has_side_effects=True, vmem_limit_bytes=32 << 20
        ),
    )(*(
        pltpu.with_memory_space_constraint(x, pltpu.HBM)
        for x in (sector_dims.T, term_shift, wavefunction, left_env, right_env)
    ))


def solution(mesh):
    nsec, nop = mesh.shape["sec"], mesh.shape["op"]
    return jax.shard_map(
        functools.partial(body, nsec, nop // 2),
        mesh=mesh,
        in_specs=(
            P("sec", None, None),
            P("sec", None),
            P("op"),
            P("op", "sec", None, None),
            P("op", "sec", None, None),
        ),
        out_specs=P("sec", None, None),
        check_vma=False,
    )
```

```python
import functools

import jax
import jax.numpy as jnp
from jax import lax
from jax.experimental import pallas as pl
from jax.experimental.pallas import tpu as pltpu
from jax.sharding import PartitionSpec as P

MESH = pl.DeviceIdType.MESH
NT = (((1,), (1,)), ((), ()))


def kernel(
    nsec,
    nz,
    dims_hbm,
    shift_hbm,
    wave_ref,
    left_ref,
    right_ref,
    out_ref,
    wide,
    near,
    left,
    right,
    part,
    sib,
    packed,
    landed,
    done,
    dims_ref,
    shift_ref,
    small_sem,
    wave_sem,
    left_sem,
    right_sem,
    halo_send,
    halo_recv,
    sib_send,
    sib_recv,
    rs_send,
    rs_recv,
    ag_send,
    ag_recv,
    share_send,
    share_recv,
    ready,
):
    order = wide.shape[1]
    terms = left.shape[1]
    rows = order // nz
    sec = lax.axis_index("sec")
    me = lax.axis_index("op")
    z = lax.div(me, 2)
    c = lax.rem(me, 2)

    def peer(d):
        return {"op": lax.rem(z + d, nz) * 2 + 1}

    sibling = {"op": z * 2 + 1 - c}
    near_z = (1, 2, nz - 2, nz - 1)

    def beside(d, core):
        return {"sec": lax.rem(sec + d + nsec, nsec), "op": z * 2 + core}

    before = lax.div(sec + nsec - 1, nsec)
    after = lax.div(2 * nsec - 2 - sec, nsec)

    def sector_of(p, e):
        return 1 - p + e * (1 + 2 * p)

    def load(it):
        q = lax.rem(it, 2)
        s = sector_of(lax.div(it, 2), q * c + (1 - q) * (1 - c))
        return (
            pltpu.make_async_copy(left_ref.at[:, s], left.at[it], left_sem.at[it]),
            pltpu.make_async_copy(right_ref.at[:, s], right.at[it], right_sem.at[it]),
        )

    def load_wave(s):
        return pltpu.make_async_copy(wave_ref.at[s], wide.at[s + 1], wave_sem.at[s])

    load_dims = pltpu.make_async_copy(dims_hbm, dims_ref, small_sem.at[0])
    load_shift = pltpu.make_async_copy(shift_hbm, shift_ref, small_sem.at[1])
    load_dims.start()
    for s in (3, 0, 1, 2):
        load_wave(s).start()
    load_shift.start()
    for copy in load(0):
        copy.start()

    barrier = pltpu.get_barrier_semaphore()

    def signal(sem, device):
        pl.semaphore_signal(sem, inc=1, device_id=device, device_id_type=MESH)

    signal(barrier, sibling)

    @pl.when(c == 1)
    def _():
        @pl.when(before == 1)
        def _():
            signal(barrier, beside(-1, 1))

        for d in near_z:
            signal(barrier, peer(d))
            signal(barrier, {"op": lax.rem(z + d, nz) * 2})

    @pl.when((c == 0) & (after == 1))
    def _():
        signal(barrier, beside(1, 1))

    def masked(block, s, start):
        row = lax.broadcasted_iota(jnp.int32, block.shape, 0) + start
        col = lax.broadcasted_iota(jnp.int32, block.shape, 1)
        keep = (row < dims_ref[0, s]) & (col < dims_ref[1, s])
        return jnp.where(keep, block, 0.0).astype(jnp.bfloat16)

    def mask(s):
        wide[s + 1] = masked(wide[s + 1].astype(jnp.float32), s, 0)

    load_dims.wait()
    for s in (3, 0):
        load_wave(s).wait()
        mask(s)
    pl.semaphore_wait(barrier, 5 + c * (before + after))

    def halo(i):
        return pltpu.make_async_remote_copy(
            src_ref=wide.at[4 - 3 * i],
            dst_ref=wide.at[5 * i],
            send_sem=halo_send.at[i],
            recv_sem=halo_recv.at[0],
            device_id=beside(1 - 2 * i, 1 - i),
            device_id_type=MESH,
        )

    @pl.when(c == 1)
    def _():
        @pl.when(before == 1)
        def _():
            halo(1).start()

        @pl.when(after == 1)
        def _():
            halo(0).start()

        for d in (2, nz - 2):
            signal(ready, peer(d))

    def passed(slot):
        return pltpu.make_async_remote_copy(
            src_ref=wide.at[slot],
            dst_ref=wide.at[slot],
            send_sem=halo_send.at[2],
            recv_sem=halo_recv.at[1],
            device_id=sibling,
            device_id_type=MESH,
        )

    for s in (1, 2):
        load_wave(s).wait()
        mask(s)
    load_shift.wait()

    def to_sibling(p):
        return pltpu.make_async_remote_copy(
            src_ref=part.at[2 * p],
            dst_ref=sib.at[p],
            send_sem=sib_send.at[p],
            recv_sem=sib_recv.at[p],
            device_id=sibling,
            device_id_type=MESH,
        )

    def scatter(p, d):
        chunk = lax.rem(z + d, nz) * rows
        return pltpu.make_async_remote_copy(
            src_ref=packed.at[p, pl.ds(pl.multiple_of(chunk, rows), rows)],
            dst_ref=landed.at[p, c * (nz - 1) + d - 1],
            send_sem=rs_send.at[p],
            recv_sem=rs_recv.at[p],
            device_id=peer(d),
            device_id_type=MESH,
        )

    mine = pl.ds(pl.multiple_of(z * rows, rows), rows)

    def hand_over(p):
        return pltpu.make_async_remote_copy(
            src_ref=packed.at[p, mine],
            dst_ref=landed.at[p, 2 * (nz - 1)],
            send_sem=rs_send.at[p],
            recv_sem=rs_recv.at[p],
            device_id=sibling,
            device_id_type=MESH,
        )

    def gather(p, d):
        return pltpu.make_async_remote_copy(
            src_ref=done.at[p, z],
            dst_ref=done.at[p, z],
            send_sem=ag_send.at[p],
            recv_sem=ag_recv.at[p, d - 1],
            device_id=peer(d),
            device_id_type=MESH,
        )

    def share(p, d):
        chunk = lax.rem(z - d + nz, nz)
        return pltpu.make_async_remote_copy(
            src_ref=done.at[p, chunk],
            dst_ref=done.at[p, chunk],
            send_sem=share_send.at[p],
            recv_sem=share_recv.at[p],
            device_id=sibling,
            device_id_type=MESH,
        )

    def wait_all(ref, sem):
        pltpu.make_async_copy(ref, ref, sem).wait()

    far = sorted(range(1, nz), key=lambda d: -min(d, nz - d))

    def step(it, carry):
        p = lax.div(it, 2)
        q = lax.rem(it, 2)
        e = q * c + (1 - q) * (1 - c)
        s = sector_of(p, e)

        @pl.when(it == 2)
        def _():
            @pl.when(c * before + (1 - c) * after == 1)
            def _():
                halo(1 - c).wait_recv()

            @pl.when(c * before + (1 - c) * after == 0)
            def _():
                wide[5 - 5 * c] = jnp.zeros((order, order), jnp.bfloat16)

            passed(5 - 5 * c).start()

        @pl.when(it == 3)
        def _():
            passed(5 * c).wait_recv()

        for n in range(3):
            near[n] = wide[s + n]
        left_now, right_now = load(it)

        @pl.when(it == 0)
        def _():
            for later in range(1, 4):
                for copy in load(later):
                    copy.start()

        left_now.wait()
        right_now.wait()

        def first(k):
            return jnp.dot(
                left[it, k], near[shift_ref[k] + 1], preferred_element_type=jnp.float32
            ).astype(jnp.bfloat16)

        total, ahead = None, first(0)
        for k in range(terms):
            now, ahead = ahead, first(k + 1) if k + 1 < terms else None
            term = lax.dot_general(now, right[it, k], NT, preferred_element_type=jnp.float32)
            total = term if total is None else total + term
        part[it] = total

        @pl.when(q == 0)
        def _():
            to_sibling(p).start()

        @pl.when(q == 1)
        def _():
            to_sibling(p).wait_recv()
            packed[p] = (total + sib[p]).astype(jnp.bfloat16)

            @pl.when(p == 0)
            def _():
                pl.semaphore_wait(ready, 1 + c)

                @pl.when(c == 1)
                def _():
                    signal(ready, sibling)

            for d in far:
                scatter(p, d).start()

            @pl.when(c == 0)
            def _():
                hand_over(p).start()

        return carry

    lax.fori_loop(0, 4, step, 0)

    def reduce(p, carry):
        mine_now = part[2 * p + 1, mine] + sib[p, mine]
        wait_all(landed.at[p], rs_recv.at[p])
        sums = [landed[p, 2 * (nz - 1)].astype(jnp.float32), mine_now]
        for d in range(1, nz):
            for core in range(2):
                sums[core] += landed[p, core * (nz - 1) + d - 1].astype(jnp.float32)
        for core in range(2):
            done[p, z, core] = masked(sums[core], sector_of(p, core), z * rows)
        for d in far:
            gather(p, d).start()
        share(p, 0).start()
        return carry

    def pass_on(p, carry):
        for d in reversed(far):
            gather(p, d).wait_recv()
            share(p, d).start()
        return carry

    def place(p):
        for core in range(2):
            for n in range(nz):
                out_ref[sector_of(p, core), pl.ds(n * rows, rows)] = done[p, n, core]

    @pl.when(c == 1)
    def _():
        lax.fori_loop(0, 2, reduce, 0)
        lax.fori_loop(0, 2, pass_on, 0)

    def finish(p, carry):
        to_sibling(p).wait_send()

        @pl.when(c == 0)
        def _():
            wait_all(packed.at[p], rs_send.at[p])
            wait_all(done.at[p], share_recv.at[p])

        place(p)

        @pl.when(c == 1)
        def _():
            wait_all(landed.at[p, pl.ds(0, nz - 1)], rs_send.at[p])
            wait_all(done.at[p, pl.ds(0, nz - 1)], ag_send.at[p])
            wait_all(done.at[p], share_send.at[p])

        return carry

    passed(5 - 5 * c).wait_send()

    @pl.when((c == 1) & (before == 1))
    def _():
        halo(1).wait_send()

    @pl.when((c == 1) & (after == 1))
    def _():
        halo(0).wait_send()

    lax.fori_loop(0, 2, finish, 0)


def body(nsec, nz, wavefunction, sector_dims, term_shift, left_env, right_env):
    count, order, _ = wavefunction.shape
    terms = left_env.shape[0]
    rows = order // nz
    bf16, f32 = jnp.bfloat16, jnp.float32
    dma = pltpu.SemaphoreType.DMA
    hbm = pl.BlockSpec(memory_space=pltpu.HBM)
    return pl.pallas_call(
        functools.partial(kernel, nsec, nz),
        out_shape=pltpu.VMEM((count, order, order), bf16),
        in_specs=[hbm] * 5,
        out_specs=pl.BlockSpec(memory_space=pltpu.VMEM),
        scratch_shapes=[
            pltpu.VMEM((count + 2, order, order), bf16),
            pltpu.VMEM((3, order, order), bf16),
            pltpu.VMEM((count, terms, order, order), bf16),
            pltpu.VMEM((count, terms, order, order), bf16),
            pltpu.VMEM((count, order, order), f32),
            pltpu.VMEM((2, order, order), f32),
            pltpu.VMEM((2, order, order), bf16),
            pltpu.VMEM((2, 2 * nz - 1, rows, order), bf16),
            pltpu.VMEM((2, nz, 2, rows, order), bf16),
            pltpu.SMEM((2, count), jnp.int32),
            pltpu.SMEM((terms,), jnp.int32),
            dma((2,)),
            dma((count,)),
            dma((count,)),
            dma((count,)),
            dma((3,)),
            dma((2,)),
            dma((2,)),
            dma((2,)),
            dma((2,)),
            dma((2,)),
            dma((2,)),
            dma((2, nz - 1)),
            dma((2,)),
            dma((2,)),
            pltpu.SemaphoreType.REGULAR,
        ],
        compiler_params=pltpu.CompilerParams(
            collective_id=0, has_side_effects=True, vmem_limit_bytes=32 << 20
        ),
    )(*(
        pltpu.with_memory_space_constraint(x, pltpu.HBM)
        for x in (sector_dims.T, term_shift, wavefunction, left_env, right_env)
    ))


def solution(mesh):
    nsec, nop = mesh.shape["sec"], mesh.shape["op"]
    return jax.shard_map(
        functools.partial(body, nsec, nop // 2),
        mesh=mesh,
        in_specs=(
            P("sec", None, None),
            P("sec", None),
            P("op"),
            P("op", "sec", None, None),
            P("op", "sec", None, None),
        ),
        out_specs=P("sec", None, None),
        check_vma=False,
    )
```

```python
import functools

import jax
import jax.numpy as jnp
from jax import lax
from jax.experimental import pallas as pl
from jax.experimental.pallas import tpu as pltpu
from jax.sharding import PartitionSpec as P

MESH = pl.DeviceIdType.MESH
NT = (((1,), (1,)), ((), ()))
ROW = 4


def kernel(
    nsec,
    nz,
    dims_hbm,
    shift_hbm,
    wave_ref,
    left_ref,
    right_ref,
    out_ref,
    wide,
    near,
    left,
    right,
    part,
    lent,
    sib,
    packed,
    landed,
    done,
    dims_ref,
    shift_ref,
    small_sem,
    wave_sem,
    left_sem,
    right_sem,
    halo_send,
    halo_recv,
    sib_send,
    sib_recv,
    rs_send,
    rs_recv,
    ag_send,
    ag_recv,
    share_send,
    share_recv,
    ready,
):
    order = wide.shape[1]
    terms = left.shape[1]
    rows = order // nz
    sec = lax.axis_index("sec")
    me = lax.axis_index("op")
    z = lax.div(me, 2)
    c = lax.rem(me, 2)

    def peer(d):
        return {"op": lax.rem(z + d, nz) * 2 + 1}

    sibling = {"op": z * 2 + 1 - c}
    far = sorted(range(1, nz), key=lambda d: -min(d, nz - d))

    def beside(d, core):
        return {"sec": lax.rem(sec + d + nsec, nsec), "op": z * 2 + core}

    before = lax.div(sec + nsec - 1, nsec)
    after = lax.div(2 * nsec - 2 - sec, nsec)

    def turned(at):
        return lax.div(lax.rem(at, ROW) + 1, ROW)

    def role(e, turn):
        return e + turn - 2 * e * turn

    r = role(c, turned(sec))

    def sector_of(p, e):
        return (1 - p) * (1 + e) + 3 * p * role(e, turned(sec))

    def load(it):
        q = lax.rem(it, 2)
        s = sector_of(lax.div(it, 2), q * c + (1 - q) * (1 - c))
        return (
            pltpu.make_async_copy(left_ref.at[:, s], left.at[it], left_sem.at[it]),
            pltpu.make_async_copy(right_ref.at[:, s], right.at[it], right_sem.at[it]),
        )

    def load_wave(s):
        return pltpu.make_async_copy(wave_ref.at[s], wide.at[s + 1], wave_sem.at[s])

    barrier = pltpu.get_barrier_semaphore()

    def signal(sem, device):
        pl.semaphore_signal(sem, inc=1, device_id=device, device_id_type=MESH)

    @pl.when((r == 1) & (before == 1))
    def _():
        signal(barrier, beside(-1, 1))

    @pl.when((r == 0) & (after == 1))
    def _():
        signal(barrier, beside(1, 1))

    signal(barrier, sibling)

    @pl.when(c == 1)
    def _():
        for d in far:
            signal(barrier, {"op": lax.rem(z + d, nz) * 2})

    load_dims = pltpu.make_async_copy(dims_hbm, dims_ref, small_sem.at[0])
    load_shift = pltpu.make_async_copy(shift_hbm, shift_ref, small_sem.at[1])
    load_dims.start()
    for s in (3, 0, 1, 2):
        load_wave(s).start()
    load_shift.start()
    for copy in load(0):
        copy.start()

    def masked(block, s, start):
        row = lax.broadcasted_iota(jnp.int32, block.shape, 0) + start
        col = lax.broadcasted_iota(jnp.int32, block.shape, 1)
        keep = (row < dims_ref[0, s]) & (col < dims_ref[1, s])
        return jnp.where(keep, block, 0.0).astype(jnp.bfloat16)

    def mask(s):
        wide[s + 1] = masked(wide[s + 1].astype(jnp.float32), s, 0)

    load_dims.wait()
    for s in (3, 0):
        load_wave(s).wait()
        mask(s)

    def halo(i):
        return pltpu.make_async_remote_copy(
            src_ref=wide.at[4 - 3 * i],
            dst_ref=wide.at[5 * i],
            send_sem=halo_send.at[i],
            recv_sem=halo_recv.at[0],
            device_id=beside(1 - 2 * i, role(1 - i, turned(sec + 1 - 2 * i + nsec))),
            device_id_type=MESH,
        )

    @pl.when(c == 1)
    def _():
        pl.semaphore_wait(barrier, 1 + before + after)

        @pl.when(before == 1)
        def _():
            halo(1).start()

        @pl.when(after == 1)
        def _():
            halo(0).start()

    def passed(slot):
        return pltpu.make_async_remote_copy(
            src_ref=wide.at[slot],
            dst_ref=wide.at[slot],
            send_sem=halo_send.at[2],
            recv_sem=halo_recv.at[1],
            device_id=sibling,
            device_id_type=MESH,
        )

    for s in (1, 2):
        load_wave(s).wait()
        mask(s)
    load_shift.wait()

    def to_sibling(p):
        return pltpu.make_async_remote_copy(
            src_ref=lent.at[p],
            dst_ref=sib.at[p],
            send_sem=sib_send.at[p],
            recv_sem=sib_recv.at[p],
            device_id=sibling,
            device_id_type=MESH,
        )

    def scatter(p, d):
        chunk = lax.rem(z + d, nz) * rows
        return pltpu.make_async_remote_copy(
            src_ref=packed.at[p, pl.ds(pl.multiple_of(chunk, rows), rows)],
            dst_ref=landed.at[p, c * (nz - 1) + d - 1],
            send_sem=rs_send.at[p],
            recv_sem=rs_recv.at[p],
            device_id=peer(d),
            device_id_type=MESH,
        )

    mine = pl.ds(pl.multiple_of(z * rows, rows), rows)

    def hand_over(p):
        return pltpu.make_async_remote_copy(
            src_ref=packed.at[p, mine],
            dst_ref=landed.at[p, 2 * (nz - 1)],
            send_sem=rs_send.at[p],
            recv_sem=rs_recv.at[p],
            device_id=sibling,
            device_id_type=MESH,
        )

    def gather(p, d):
        return pltpu.make_async_remote_copy(
            src_ref=done.at[p, z],
            dst_ref=done.at[p, z],
            send_sem=ag_send.at[p],
            recv_sem=ag_recv.at[p, d - 1],
            device_id=peer(d),
            device_id_type=MESH,
        )

    def share(p, d):
        chunk = lax.rem(z - d + nz, nz)
        return pltpu.make_async_remote_copy(
            src_ref=done.at[p, chunk],
            dst_ref=done.at[p, chunk],
            send_sem=share_send.at[p],
            recv_sem=share_recv.at[p],
            device_id=sibling,
            device_id_type=MESH,
        )

    def wait_all(ref, sem):
        pltpu.make_async_copy(ref, ref, sem).wait()

    def step(it, carry):
        p = lax.div(it, 2)
        q = lax.rem(it, 2)
        e = q * c + (1 - q) * (1 - c)
        s = sector_of(p, e)

        @pl.when(it == 2)
        def _():
            @pl.when(r * before + (1 - r) * after == 1)
            def _():
                halo(1 - r).wait_recv()

            @pl.when(r * before + (1 - r) * after == 0)
            def _():
                wide[5 - 5 * r] = jnp.zeros((order, order), jnp.bfloat16)

            passed(5 - 5 * r).start()

        @pl.when(it == 3)
        def _():
            passed(5 * r).wait_recv()

        for n in range(3):
            near[n] = wide[s + n]
        left_now, right_now = load(it)

        @pl.when(it == 0)
        def _():
            for later in range(1, 4):
                for copy in load(later):
                    copy.start()

        left_now.wait()
        right_now.wait()

        def first(k):
            return jnp.dot(
                left[it, k], near[shift_ref[k] + 1], preferred_element_type=jnp.float32
            ).astype(jnp.bfloat16)

        total, ahead = None, first(0)
        for k in range(terms):
            now, ahead = ahead, first(k + 1) if k + 1 < terms else None
            term = lax.dot_general(now, right[it, k], NT, preferred_element_type=jnp.float32)
            total = term if total is None else total + term

        @pl.when((it == 0) & (c == 0))
        def _():
            pl.semaphore_wait(barrier, nz)
            signal(ready, sibling)

        @pl.when(q == 0)
        def _():
            lent[p] = total.astype(jnp.bfloat16)
            to_sibling(p).start()

        @pl.when(q == 1)
        def _():
            to_sibling(p).wait_recv()
            both = total + sib[p].astype(jnp.float32)
            part[p] = both
            packed[p] = both.astype(jnp.bfloat16)

            @pl.when((p == 0) & (c == 1))
            def _():
                pl.semaphore_wait(ready, 1)

            for d in far:
                scatter(p, d).start()

            @pl.when(c == 0)
            def _():
                hand_over(p).start()

        return carry

    lax.fori_loop(0, 4, step, 0)

    def reduce(p, carry):
        mine_now = part[p, mine]
        wait_all(landed.at[p], rs_recv.at[p])
        sums = [landed[p, 2 * (nz - 1)].astype(jnp.float32), mine_now]
        for d in range(1, nz):
            for core in range(2):
                sums[core] += landed[p, core * (nz - 1) + d - 1].astype(jnp.float32)
        for core in range(2):
            done[p, z, core] = masked(sums[core], sector_of(p, core), z * rows)
        for d in far:
            gather(p, d).start()
        share(p, 0).start()
        return carry

    def pass_on(p, carry):
        for d in reversed(far):
            gather(p, d).wait_recv()
            share(p, d).start()
        return carry

    def place(p):
        for core in range(2):
            for n in range(nz):
                out_ref[sector_of(p, core), pl.ds(n * rows, rows)] = done[p, n, core]

    @pl.when(c == 1)
    def _():
        lax.fori_loop(0, 2, reduce, 0)
        lax.fori_loop(0, 2, pass_on, 0)

    def finish(p, carry):
        to_sibling(p).wait_send()

        @pl.when(c == 0)
        def _():
            wait_all(packed.at[p], rs_send.at[p])
            wait_all(done.at[p], share_recv.at[p])

        place(p)

        @pl.when(c == 1)
        def _():
            wait_all(landed.at[p, pl.ds(0, nz - 1)], rs_send.at[p])
            wait_all(done.at[p, pl.ds(0, nz - 1)], ag_send.at[p])
            wait_all(done.at[p], share_send.at[p])

        return carry

    passed(5 - 5 * r).wait_send()

    @pl.when((c == 1) & (before == 1))
    def _():
        halo(1).wait_send()

    @pl.when((c == 1) & (after == 1))
    def _():
        halo(0).wait_send()

    lax.fori_loop(0, 2, finish, 0)


def body(nsec, nz, wavefunction, sector_dims, term_shift, left_env, right_env):
    count, order, _ = wavefunction.shape
    terms = left_env.shape[0]
    rows = order // nz
    bf16, f32 = jnp.bfloat16, jnp.float32
    dma = pltpu.SemaphoreType.DMA
    hbm = pl.BlockSpec(memory_space=pltpu.HBM)
    return pl.pallas_call(
        functools.partial(kernel, nsec, nz),
        out_shape=pltpu.VMEM((count, order, order), bf16),
        in_specs=[hbm] * 5,
        out_specs=pl.BlockSpec(memory_space=pltpu.VMEM),
        scratch_shapes=[
            pltpu.VMEM((count + 2, order, order), bf16),
            pltpu.VMEM((3, order, order), bf16),
            pltpu.VMEM((count, terms, order, order), bf16),
            pltpu.VMEM((count, terms, order, order), bf16),
            pltpu.VMEM((2, order, order), f32),
            pltpu.VMEM((2, order, order), bf16),
            pltpu.VMEM((2, order, order), bf16),
            pltpu.VMEM((2, order, order), bf16),
            pltpu.VMEM((2, 2 * nz - 1, rows, order), bf16),
            pltpu.VMEM((2, nz, 2, rows, order), bf16),
            pltpu.SMEM((2, count), jnp.int32),
            pltpu.SMEM((terms,), jnp.int32),
            dma((2,)),
            dma((count,)),
            dma((count,)),
            dma((count,)),
            dma((3,)),
            dma((2,)),
            dma((2,)),
            dma((2,)),
            dma((2,)),
            dma((2,)),
            dma((2,)),
            dma((2, nz - 1)),
            dma((2,)),
            dma((2,)),
            pltpu.SemaphoreType.REGULAR,
        ],
        compiler_params=pltpu.CompilerParams(
            collective_id=0, has_side_effects=True, vmem_limit_bytes=32 << 20
        ),
    )(*(
        pltpu.with_memory_space_constraint(x, pltpu.HBM)
        for x in (sector_dims.T, term_shift, wavefunction, left_env, right_env)
    ))


def solution(mesh):
    nsec, nop = mesh.shape["sec"], mesh.shape["op"]
    return jax.shard_map(
        functools.partial(body, nsec, nop // 2),
        mesh=mesh,
        in_specs=(
            P("sec", None, None),
            P("sec", None),
            P("op"),
            P("op", "sec", None, None),
            P("op", "sec", None, None),
        ),
        out_specs=P("sec", None, None),
        check_vma=False,
    )
```

```python
import functools

import jax
import jax.numpy as jnp
from jax import lax
from jax.experimental import pallas as pl
from jax.experimental.pallas import tpu as pltpu
from jax.sharding import PartitionSpec as P

MESH = pl.DeviceIdType.MESH
NT = (((1,), (1,)), ((), ()))
ROW = 4


def kernel(
    nsec,
    nz,
    dims_hbm,
    shift_hbm,
    wave_ref,
    left_ref,
    right_ref,
    out_ref,
    wide,
    near,
    left,
    right,
    part,
    lent,
    sib,
    packed,
    landed,
    done,
    dims_ref,
    shift_ref,
    small_sem,
    wave_sem,
    left_sem,
    right_sem,
    halo_send,
    halo_recv,
    sib_send,
    sib_recv,
    rs_send,
    rs_recv,
    ag_send,
    ag_recv,
    share_send,
    share_recv,
    ready,
):
    order = wide.shape[1]
    terms = left.shape[1]
    rows = order // nz
    sec = lax.axis_index("sec")
    me = lax.axis_index("op")
    z = lax.div(me, 2)
    c = lax.rem(me, 2)

    def peer(d, core):
        return {"op": lax.rem(z + d, nz) * 2 + core}

    sibling = {"op": z * 2 + 1 - c}
    far = sorted(range(1, nz), key=lambda d: -min(d, nz - d))

    def beside(d, core):
        return {"sec": lax.rem(sec + d + nsec, nsec), "op": z * 2 + core}

    before = lax.div(sec + nsec - 1, nsec)
    after = lax.div(2 * nsec - 2 - sec, nsec)

    def turned(at):
        return lax.div(lax.rem(at, ROW) + 1, ROW)

    def role(e, turn):
        return e + turn - 2 * e * turn

    r = role(c, turned(sec))

    def sector_of(p, e):
        return (1 - p) * (1 + e) + 3 * p * role(e, turned(sec))

    def load(it):
        q = lax.rem(it, 2)
        s = sector_of(lax.div(it, 2), q * c + (1 - q) * (1 - c))
        return (
            pltpu.make_async_copy(left_ref.at[:, s], left.at[it], left_sem.at[it]),
            pltpu.make_async_copy(right_ref.at[:, s], right.at[it], right_sem.at[it]),
        )

    def load_wave(s):
        return pltpu.make_async_copy(wave_ref.at[s], wide.at[s + 1], wave_sem.at[s])

    barrier = pltpu.get_barrier_semaphore()

    def signal(sem, device):
        pl.semaphore_signal(sem, inc=1, device_id=device, device_id_type=MESH)

    @pl.when((r == 1) & (before == 1))
    def _():
        signal(barrier, beside(-1, 1))

    @pl.when((r == 0) & (after == 1))
    def _():
        signal(barrier, beside(1, 1))

    load_dims = pltpu.make_async_copy(dims_hbm, dims_ref, small_sem.at[0])
    load_shift = pltpu.make_async_copy(shift_hbm, shift_ref, small_sem.at[1])
    load_dims.start()
    for s in (3, 0, 1, 2):
        load_wave(s).start()
    signal(barrier, sibling)

    for d in far:
        signal(barrier, peer(d, 0))

    load_shift.start()
    for copy in load(0):
        copy.start()

    def masked(block, s, start):
        row = lax.broadcasted_iota(jnp.int32, block.shape, 0) + start
        col = lax.broadcasted_iota(jnp.int32, block.shape, 1)
        keep = (row < dims_ref[0, s]) & (col < dims_ref[1, s])
        return jnp.where(keep, block, 0.0).astype(jnp.bfloat16)

    def mask(s):
        wide[s + 1] = masked(wide[s + 1].astype(jnp.float32), s, 0)

    load_dims.wait()
    load_wave(3).wait()
    mask(3)

    def halo(i):
        return pltpu.make_async_remote_copy(
            src_ref=wide.at[4 - 3 * i],
            dst_ref=wide.at[5 * i],
            send_sem=halo_send.at[i],
            recv_sem=halo_recv.at[0],
            device_id=beside(1 - 2 * i, role(1 - i, turned(sec + 1 - 2 * i + nsec))),
            device_id_type=MESH,
        )

    @pl.when(c == 1)
    def _():
        pl.semaphore_wait(barrier, 1 + before + after)
        signal(ready, sibling)

        @pl.when(after == 1)
        def _():
            halo(0).start()

    load_wave(0).wait()
    mask(0)

    @pl.when((c == 1) & (before == 1))
    def _():
        halo(1).start()

    def passed(slot):
        return pltpu.make_async_remote_copy(
            src_ref=wide.at[slot],
            dst_ref=wide.at[slot],
            send_sem=halo_send.at[2],
            recv_sem=halo_recv.at[1],
            device_id=sibling,
            device_id_type=MESH,
        )

    for s in (1, 2):
        load_wave(s).wait()
        mask(s)
    load_shift.wait()

    def to_sibling(p):
        return pltpu.make_async_remote_copy(
            src_ref=lent.at[p],
            dst_ref=sib.at[p],
            send_sem=sib_send.at[p],
            recv_sem=sib_recv.at[p],
            device_id=sibling,
            device_id_type=MESH,
        )

    def scatter(p, d):
        chunk = lax.rem(z + d, nz) * rows
        return pltpu.make_async_remote_copy(
            src_ref=packed.at[p, pl.ds(pl.multiple_of(chunk, rows), rows)],
            dst_ref=landed.at[p, c * (nz - 1) + d - 1],
            send_sem=rs_send.at[p],
            recv_sem=rs_recv.at[p],
            device_id=peer(d, p),
            device_id_type=MESH,
        )

    mine = pl.ds(pl.multiple_of(z * rows, rows), rows)

    def hand_over(p):
        return pltpu.make_async_remote_copy(
            src_ref=packed.at[p, mine],
            dst_ref=landed.at[p, 2 * (nz - 1)],
            send_sem=rs_send.at[p],
            recv_sem=rs_recv.at[p],
            device_id=sibling,
            device_id_type=MESH,
        )

    def gather(p, d):
        return pltpu.make_async_remote_copy(
            src_ref=done.at[p, z],
            dst_ref=done.at[p, z],
            send_sem=ag_send.at[p],
            recv_sem=ag_recv.at[p, d - 1],
            device_id=peer(d, p),
            device_id_type=MESH,
        )

    def share(p, d):
        chunk = lax.rem(z - d + nz, nz)
        return pltpu.make_async_remote_copy(
            src_ref=done.at[p, chunk],
            dst_ref=done.at[p, chunk],
            send_sem=share_send.at[p],
            recv_sem=share_recv.at[p],
            device_id=sibling,
            device_id_type=MESH,
        )

    def wait_all(ref, sem):
        pltpu.make_async_copy(ref, ref, sem).wait()

    def step(it, carry):
        p = lax.div(it, 2)
        q = lax.rem(it, 2)
        e = q * c + (1 - q) * (1 - c)
        s = sector_of(p, e)

        @pl.when(it == 2)
        def _():
            @pl.when(r * before + (1 - r) * after == 1)
            def _():
                halo(1 - r).wait_recv()

            @pl.when(r * before + (1 - r) * after == 0)
            def _():
                wide[5 - 5 * r] = jnp.zeros((order, order), jnp.bfloat16)

            passed(5 - 5 * r).start()

        @pl.when(it == 3)
        def _():
            passed(5 * r).wait_recv()

        for n in range(3):
            near[n] = wide[s + n]
        left_now, right_now = load(it)

        @pl.when(it == 0)
        def _():
            for later in range(1, 4):
                for copy in load(later):
                    copy.start()

        left_now.wait()
        right_now.wait()

        def first(k):
            return jnp.dot(
                left[it, k], near[shift_ref[k] + 1], preferred_element_type=jnp.float32
            ).astype(jnp.bfloat16)

        total, ahead = None, first(0)
        for k in range(terms):
            now, ahead = ahead, first(k + 1) if k + 1 < terms else None
            term = lax.dot_general(now, right[it, k], NT, preferred_element_type=jnp.float32)
            total = term if total is None else total + term

        @pl.when((it == 0) & (c == 0))
        def _():
            pl.semaphore_wait(ready, 1)

        @pl.when(q == 0)
        def _():
            lent[p] = total.astype(jnp.bfloat16)
            to_sibling(p).start()

        @pl.when(q == 1)
        def _():
            to_sibling(p).wait_recv()
            both = total + sib[p].astype(jnp.float32)
            part[p] = both
            packed[p] = both.astype(jnp.bfloat16)

            @pl.when((p == 0) & (c == 0))
            def _():
                pl.semaphore_wait(barrier, 2 * nz - 1)
                signal(ready, sibling)

            @pl.when((p == 0) & (c == 1))
            def _():
                pl.semaphore_wait(ready, 1)

            for d in far:
                scatter(p, d).start()

            @pl.when(c != p)
            def _():
                hand_over(p).start()

        return carry

    lax.fori_loop(0, 4, step, 0)

    def reduce(p):
        mine_now = part[p, mine]
        wait_all(landed.at[p], rs_recv.at[p])
        given = landed[p, 2 * (nz - 1)].astype(jnp.float32)
        sums = [jnp.where(p == core, mine_now, given) for core in range(2)]
        for d in range(1, nz):
            for core in range(2):
                sums[core] += landed[p, core * (nz - 1) + d - 1].astype(jnp.float32)
        for core in range(2):
            done[p, z, core] = masked(sums[core], sector_of(p, core), z * rows)
        for d in far:
            gather(p, d).start()
        share(p, 0).start()

    def pass_on(p):
        for d in reversed(far):
            gather(p, d).wait_recv()
            share(p, d).start()

    def place(p):
        for core in range(2):
            for n in range(nz):
                out_ref[sector_of(p, core), pl.ds(n * rows, rows)] = done[p, n, core]

    reduce(c)
    pass_on(c)

    def finish(p, carry):
        to_sibling(p).wait_send()

        @pl.when(c != p)
        def _():
            wait_all(packed.at[p], rs_send.at[p])
            wait_all(done.at[p], share_recv.at[p])

        place(p)

        @pl.when(c == p)
        def _():
            wait_all(landed.at[p, pl.ds(0, nz - 1)], rs_send.at[p])
            wait_all(done.at[p, pl.ds(0, nz - 1)], ag_send.at[p])
            wait_all(done.at[p], share_send.at[p])

        return carry

    passed(5 - 5 * r).wait_send()

    @pl.when((c == 1) & (before == 1))
    def _():
        halo(1).wait_send()

    @pl.when((c == 1) & (after == 1))
    def _():
        halo(0).wait_send()

    lax.fori_loop(0, 2, finish, 0)


def body(nsec, nz, wavefunction, sector_dims, term_shift, left_env, right_env):
    count, order, _ = wavefunction.shape
    terms = left_env.shape[0]
    rows = order // nz
    bf16, f32 = jnp.bfloat16, jnp.float32
    dma = pltpu.SemaphoreType.DMA
    hbm = pl.BlockSpec(memory_space=pltpu.HBM)
    return pl.pallas_call(
        functools.partial(kernel, nsec, nz),
        out_shape=pltpu.VMEM((count, order, order), bf16),
        in_specs=[hbm] * 5,
        out_specs=pl.BlockSpec(memory_space=pltpu.VMEM),
        scratch_shapes=[
            pltpu.VMEM((count + 2, order, order), bf16),
            pltpu.VMEM((3, order, order), bf16),
            pltpu.VMEM((count, terms, order, order), bf16),
            pltpu.VMEM((count, terms, order, order), bf16),
            pltpu.VMEM((2, order, order), f32),
            pltpu.VMEM((2, order, order), bf16),
            pltpu.VMEM((2, order, order), bf16),
            pltpu.VMEM((2, order, order), bf16),
            pltpu.VMEM((2, 2 * nz - 1, rows, order), bf16),
            pltpu.VMEM((2, nz, 2, rows, order), bf16),
            pltpu.SMEM((2, count), jnp.int32),
            pltpu.SMEM((terms,), jnp.int32),
            dma((2,)),
            dma((count,)),
            dma((count,)),
            dma((count,)),
            dma((3,)),
            dma((2,)),
            dma((2,)),
            dma((2,)),
            dma((2,)),
            dma((2,)),
            dma((2,)),
            dma((2, nz - 1)),
            dma((2,)),
            dma((2,)),
            pltpu.SemaphoreType.REGULAR,
        ],
        compiler_params=pltpu.CompilerParams(
            collective_id=0, has_side_effects=True, vmem_limit_bytes=32 << 20
        ),
    )(*(
        pltpu.with_memory_space_constraint(x, pltpu.HBM)
        for x in (sector_dims.T, term_shift, wavefunction, left_env, right_env)
    ))


def solution(mesh):
    nsec, nop = mesh.shape["sec"], mesh.shape["op"]
    return jax.shard_map(
        functools.partial(body, nsec, nop // 2),
        mesh=mesh,
        in_specs=(
            P("sec", None, None),
            P("sec", None),
            P("op"),
            P("op", "sec", None, None),
            P("op", "sec", None, None),
        ),
        out_specs=P("sec", None, None),
        check_vma=False,
    )
```

```python
import functools

import jax
import jax.numpy as jnp
from jax import lax
from jax.experimental import pallas as pl
from jax.experimental.pallas import tpu as pltpu
from jax.sharding import PartitionSpec as P

MESH = pl.DeviceIdType.MESH
NT = (((1,), (1,)), ((), ()))
ROW = 4


def kernel(
    nsec,
    nz,
    dims_hbm,
    shift_hbm,
    wave_ref,
    left_ref,
    right_ref,
    out_ref,
    wide,
    near,
    left,
    right,
    part,
    lent,
    sib,
    packed,
    landed,
    done,
    dims_ref,
    shift_ref,
    small_sem,
    wave_sem,
    left_sem,
    right_sem,
    halo_send,
    halo_recv,
    sib_send,
    sib_recv,
    rs_send,
    rs_recv,
    ag_send,
    ag_recv,
    share_send,
    share_recv,
    ready,
):
    order = wide.shape[1]
    terms = left.shape[1]
    rows = order // nz
    sec = lax.axis_index("sec")
    me = lax.axis_index("op")
    z = lax.div(me, 2)
    c = lax.rem(me, 2)

    def peer(d, core):
        return {"op": lax.rem(z + d, nz) * 2 + core}

    sibling = {"op": z * 2 + 1 - c}
    far = sorted(range(1, nz), key=lambda d: -min(d, nz - d))

    def beside(d, core):
        return {"sec": lax.rem(sec + d + nsec, nsec), "op": z * 2 + core}

    before = lax.div(sec + nsec - 1, nsec)
    after = lax.div(2 * nsec - 2 - sec, nsec)

    def turned(at):
        return lax.div(lax.rem(at, ROW) + 1, ROW)

    def role(e, turn):
        return e + turn - 2 * e * turn

    r = role(c, turned(sec))

    def sector_of(p, e):
        return (1 - p) * (1 + e) + 3 * p * role(e, turned(sec))

    def load(it):
        q = lax.rem(it, 2)
        s = sector_of(lax.div(it, 2), q * c + (1 - q) * (1 - c))
        return (
            pltpu.make_async_copy(left_ref.at[:, s], left.at[it], left_sem.at[it]),
            pltpu.make_async_copy(right_ref.at[:, s], right.at[it], right_sem.at[it]),
        )

    def load_wave(s):
        return pltpu.make_async_copy(wave_ref.at[s], wide.at[s + 1], wave_sem.at[s])

    barrier = pltpu.get_barrier_semaphore()

    def signal(sem, device):
        pl.semaphore_signal(sem, inc=1, device_id=device, device_id_type=MESH)

    @pl.when((r == 1) & (before == 1))
    def _():
        signal(barrier, beside(-1, 1))

    @pl.when((r == 0) & (after == 1))
    def _():
        signal(barrier, beside(1, 1))

    load_dims = pltpu.make_async_copy(dims_hbm, dims_ref, small_sem.at[0])
    load_shift = pltpu.make_async_copy(shift_hbm, shift_ref, small_sem.at[1])
    load_dims.start()
    for s in (3, 0, 1, 2):
        load_wave(s).start()
    signal(barrier, sibling)

    for d in far:
        signal(barrier, peer(d, 0))

    load_shift.start()
    for copy in load(0):
        copy.start()

    def masked(block, s, start):
        row = lax.broadcasted_iota(jnp.int32, block.shape, 0) + start
        col = lax.broadcasted_iota(jnp.int32, block.shape, 1)
        keep = (row < dims_ref[0, s]) & (col < dims_ref[1, s])
        return jnp.where(keep, block, 0.0).astype(jnp.bfloat16)

    def mask(s):
        wide[s + 1] = masked(wide[s + 1].astype(jnp.float32), s, 0)

    load_dims.wait()
    load_wave(3).wait()
    for copy in load(1):
        copy.start()
    mask(3)

    def halo(i):
        return pltpu.make_async_remote_copy(
            src_ref=wide.at[4 - 3 * i],
            dst_ref=wide.at[5 * i],
            send_sem=halo_send.at[i],
            recv_sem=halo_recv.at[0],
            device_id=beside(1 - 2 * i, role(1 - i, turned(sec + 1 - 2 * i + nsec))),
            device_id_type=MESH,
        )

    @pl.when(c == 1)
    def _():
        pl.semaphore_wait(barrier, 1 + before + after)
        signal(ready, sibling)

        @pl.when(after == 1)
        def _():
            halo(0).start()

    load_wave(0).wait()
    mask(0)

    @pl.when((c == 1) & (before == 1))
    def _():
        halo(1).start()

    def passed(slot):
        return pltpu.make_async_remote_copy(
            src_ref=wide.at[slot],
            dst_ref=wide.at[slot],
            send_sem=halo_send.at[2],
            recv_sem=halo_recv.at[1],
            device_id=sibling,
            device_id_type=MESH,
        )

    for s in (1, 2):
        load_wave(s).wait()
        mask(s)
    load_shift.wait()

    def to_sibling(p):
        return pltpu.make_async_remote_copy(
            src_ref=lent.at[p],
            dst_ref=sib.at[p],
            send_sem=sib_send.at[p],
            recv_sem=sib_recv.at[p],
            device_id=sibling,
            device_id_type=MESH,
        )

    def scatter(p, d):
        chunk = lax.rem(z + d, nz) * rows
        return pltpu.make_async_remote_copy(
            src_ref=packed.at[p, pl.ds(pl.multiple_of(chunk, rows), rows)],
            dst_ref=landed.at[p, c * (nz - 1) + d - 1],
            send_sem=rs_send.at[p],
            recv_sem=rs_recv.at[p],
            device_id=peer(d, p),
            device_id_type=MESH,
        )

    mine = pl.ds(pl.multiple_of(z * rows, rows), rows)

    def hand_over(p):
        return pltpu.make_async_remote_copy(
            src_ref=packed.at[p, mine],
            dst_ref=landed.at[p, 2 * (nz - 1)],
            send_sem=rs_send.at[p],
            recv_sem=rs_recv.at[p],
            device_id=sibling,
            device_id_type=MESH,
        )

    def gather(p, d):
        return pltpu.make_async_remote_copy(
            src_ref=done.at[p, z],
            dst_ref=done.at[p, z],
            send_sem=ag_send.at[p],
            recv_sem=ag_recv.at[p, d - 1],
            device_id=peer(d, p),
            device_id_type=MESH,
        )

    def share(p, d):
        chunk = lax.rem(z - d + nz, nz)
        return pltpu.make_async_remote_copy(
            src_ref=done.at[p, chunk],
            dst_ref=done.at[p, chunk],
            send_sem=share_send.at[p],
            recv_sem=share_recv.at[p],
            device_id=sibling,
            device_id_type=MESH,
        )

    def wait_all(ref, sem):
        pltpu.make_async_copy(ref, ref, sem).wait()

    def step(it, carry):
        p = lax.div(it, 2)
        q = lax.rem(it, 2)
        e = q * c + (1 - q) * (1 - c)
        s = sector_of(p, e)

        @pl.when(it == 2)
        def _():
            @pl.when(r * before + (1 - r) * after == 1)
            def _():
                halo(1 - r).wait_recv()

            @pl.when(r * before + (1 - r) * after == 0)
            def _():
                wide[5 - 5 * r] = jnp.zeros((order, order), jnp.bfloat16)

            passed(5 - 5 * r).start()

        @pl.when(it == 3)
        def _():
            passed(5 * r).wait_recv()

        for n in range(3):
            near[n] = wide[s + n]
        left_now, right_now = load(it)

        @pl.when(it == 0)
        def _():
            for later in range(2, 4):
                for copy in load(later):
                    copy.start()

        left_now.wait()
        right_now.wait()

        def first(k):
            return jnp.dot(
                left[it, k], near[shift_ref[k] + 1], preferred_element_type=jnp.float32
            ).astype(jnp.bfloat16)

        total, ahead = None, first(0)
        for k in range(terms):
            now, ahead = ahead, first(k + 1) if k + 1 < terms else None
            term = lax.dot_general(now, right[it, k], NT, preferred_element_type=jnp.float32)
            total = term if total is None else total + term

        @pl.when((it == 0) & (c == 0))
        def _():
            pl.semaphore_wait(ready, 1)

        @pl.when(q == 0)
        def _():
            lent[p] = total.astype(jnp.bfloat16)
            to_sibling(p).start()

        @pl.when(q == 1)
        def _():
            to_sibling(p).wait_recv()
            both = total + sib[p].astype(jnp.float32)
            part[p] = both
            packed[p] = both.astype(jnp.bfloat16)

            @pl.when((p == 0) & (c == 0))
            def _():
                pl.semaphore_wait(barrier, 2 * nz - 1)
                signal(ready, sibling)

            @pl.when((p == 0) & (c == 1))
            def _():
                pl.semaphore_wait(ready, 1)

            for d in far:
                scatter(p, d).start()

            @pl.when(c != p)
            def _():
                hand_over(p).start()

        return carry

    lax.fori_loop(0, 4, step, 0)

    def reduce(p):
        mine_now = part[p, mine]
        wait_all(landed.at[p], rs_recv.at[p])
        given = landed[p, 2 * (nz - 1)].astype(jnp.float32)
        sums = [jnp.where(p == core, mine_now, given) for core in range(2)]
        for d in range(1, nz):
            for core in range(2):
                sums[core] += landed[p, core * (nz - 1) + d - 1].astype(jnp.float32)
        for core in range(2):
            done[p, z, core] = masked(sums[core], sector_of(p, core), z * rows)
        for d in far:
            gather(p, d).start()
        share(p, 0).start()

    def pass_on(p):
        for d in reversed(far):
            gather(p, d).wait_recv()
            share(p, d).start()

    def place(p):
        for core in range(2):
            for n in range(nz):
                out_ref[sector_of(p, core), pl.ds(n * rows, rows)] = done[p, n, core]

    reduce(c)
    pass_on(c)

    def finish(p, carry):
        to_sibling(p).wait_send()

        @pl.when(c != p)
        def _():
            wait_all(packed.at[p], rs_send.at[p])
            wait_all(done.at[p], share_recv.at[p])

        place(p)

        @pl.when(c == p)
        def _():
            wait_all(landed.at[p, pl.ds(0, nz - 1)], rs_send.at[p])
            wait_all(done.at[p, pl.ds(0, nz - 1)], ag_send.at[p])
            wait_all(done.at[p], share_send.at[p])

        return carry

    passed(5 - 5 * r).wait_send()

    @pl.when((c == 1) & (before == 1))
    def _():
        halo(1).wait_send()

    @pl.when((c == 1) & (after == 1))
    def _():
        halo(0).wait_send()

    lax.fori_loop(0, 2, finish, 0)


def body(nsec, nz, wavefunction, sector_dims, term_shift, left_env, right_env):
    count, order, _ = wavefunction.shape
    terms = left_env.shape[0]
    rows = order // nz
    bf16, f32 = jnp.bfloat16, jnp.float32
    dma = pltpu.SemaphoreType.DMA
    hbm = pl.BlockSpec(memory_space=pltpu.HBM)
    return pl.pallas_call(
        functools.partial(kernel, nsec, nz),
        out_shape=pltpu.VMEM((count, order, order), bf16),
        in_specs=[hbm] * 5,
        out_specs=pl.BlockSpec(memory_space=pltpu.VMEM),
        scratch_shapes=[
            pltpu.VMEM((count + 2, order, order), bf16),
            pltpu.VMEM((3, order, order), bf16),
            pltpu.VMEM((count, terms, order, order), bf16),
            pltpu.VMEM((count, terms, order, order), bf16),
            pltpu.VMEM((2, order, order), f32),
            pltpu.VMEM((2, order, order), bf16),
            pltpu.VMEM((2, order, order), bf16),
            pltpu.VMEM((2, order, order), bf16),
            pltpu.VMEM((2, 2 * nz - 1, rows, order), bf16),
            pltpu.VMEM((2, nz, 2, rows, order), bf16),
            pltpu.SMEM((2, count), jnp.int32),
            pltpu.SMEM((terms,), jnp.int32),
            dma((2,)),
            dma((count,)),
            dma((count,)),
            dma((count,)),
            dma((3,)),
            dma((2,)),
            dma((2,)),
            dma((2,)),
            dma((2,)),
            dma((2,)),
            dma((2,)),
            dma((2, nz - 1)),
            dma((2,)),
            dma((2,)),
            pltpu.SemaphoreType.REGULAR,
        ],
        compiler_params=pltpu.CompilerParams(
            collective_id=0, has_side_effects=True, vmem_limit_bytes=32 << 20
        ),
    )(*(
        pltpu.with_memory_space_constraint(x, pltpu.HBM)
        for x in (sector_dims.T, term_shift, wavefunction, left_env, right_env)
    ))


def solution(mesh):
    nsec, nop = mesh.shape["sec"], mesh.shape["op"]
    return jax.shard_map(
        functools.partial(body, nsec, nop // 2),
        mesh=mesh,
        in_specs=(
            P("sec", None, None),
            P("sec", None),
            P("op"),
            P("op", "sec", None, None),
            P("op", "sec", None, None),
        ),
        out_specs=P("sec", None, None),
        check_vma=False,
    )
```

```python
import functools

import jax
import jax.numpy as jnp
from jax import lax
from jax.experimental import pallas as pl
from jax.experimental.pallas import tpu as pltpu
from jax.sharding import PartitionSpec as P

MESH = pl.DeviceIdType.MESH
NT = (((1,), (1,)), ((), ()))
ROW = 4


def kernel(
    nsec,
    nz,
    dims_hbm,
    shift_hbm,
    wave_ref,
    left_ref,
    right_ref,
    out_ref,
    wide,
    near,
    left,
    right,
    part,
    lent,
    sib,
    packed,
    landed,
    done,
    dims_ref,
    shift_ref,
    small_sem,
    wave_sem,
    left_sem,
    right_sem,
    halo_send,
    halo_recv,
    sib_send,
    sib_recv,
    rs_send,
    rs_recv,
    ag_send,
    ag_recv,
    share_send,
    share_recv,
    ready,
):
    order = wide.shape[1]
    terms = left.shape[1]
    rows = order // nz
    sec = lax.axis_index("sec")
    me = lax.axis_index("op")
    z = lax.div(me, 2)
    c = lax.rem(me, 2)

    def peer(d, core):
        return {"op": lax.rem(z + d, nz) * 2 + core}

    sibling = {"op": z * 2 + 1 - c}
    far = sorted(range(1, nz), key=lambda d: -min(d, nz - d))

    def beside(d, core):
        return {"sec": lax.rem(sec + d + nsec, nsec), "op": z * 2 + core}

    before = lax.div(sec + nsec - 1, nsec)
    after = lax.div(2 * nsec - 2 - sec, nsec)

    def turned(at):
        return lax.div(lax.rem(at, ROW) + 1, ROW)

    def role(e, turn):
        return e + turn - 2 * e * turn

    r = role(c, turned(sec))

    def sector_of(p, e):
        return (1 - p) * (1 + e) + 3 * p * role(e, turned(sec))

    def load(it):
        q = lax.rem(it, 2)
        s = sector_of(lax.div(it, 2), q * c + (1 - q) * (1 - c))
        return (
            pltpu.make_async_copy(left_ref.at[:, s], left.at[it], left_sem.at[it]),
            pltpu.make_async_copy(right_ref.at[:, s], right.at[it], right_sem.at[it]),
        )

    def load_wave(s):
        return pltpu.make_async_copy(wave_ref.at[s], wide.at[s + 1], wave_sem.at[s])

    barrier = pltpu.get_barrier_semaphore()

    def signal(sem, device):
        pl.semaphore_signal(sem, inc=1, device_id=device, device_id_type=MESH)

    @pl.when((r == 1) & (before == 1))
    def _():
        signal(barrier, beside(-1, 1))

    @pl.when((r == 0) & (after == 1))
    def _():
        signal(barrier, beside(1, 1))

    load_dims = pltpu.make_async_copy(dims_hbm, dims_ref, small_sem.at[0])
    load_shift = pltpu.make_async_copy(shift_hbm, shift_ref, small_sem.at[1])
    load_dims.start()
    for s in (3, 0, 1, 2):
        load_wave(s).start()
    signal(barrier, sibling)

    for d in far:
        signal(barrier, peer(d, 0))

    load_shift.start()
    for copy in load(0):
        copy.start()

    def masked(block, s, start):
        row = lax.broadcasted_iota(jnp.int32, block.shape, 0) + start
        col = lax.broadcasted_iota(jnp.int32, block.shape, 1)
        keep = (row < dims_ref[0, s]) & (col < dims_ref[1, s])
        return jnp.where(keep, block, 0.0).astype(jnp.bfloat16)

    def mask(s):
        wide[s + 1] = masked(wide[s + 1].astype(jnp.float32), s, 0)

    load_dims.wait()
    load_wave(3).wait()
    for copy in load(1):
        copy.start()
    mask(3)

    def halo(i):
        return pltpu.make_async_remote_copy(
            src_ref=wide.at[4 - 3 * i],
            dst_ref=wide.at[5 * i],
            send_sem=halo_send.at[i],
            recv_sem=halo_recv.at[0],
            device_id=beside(1 - 2 * i, role(1 - i, turned(sec + 1 - 2 * i + nsec))),
            device_id_type=MESH,
        )

    @pl.when(c == 1)
    def _():
        pl.semaphore_wait(barrier, 1 + before + after)
        signal(ready, sibling)

        @pl.when(after == 1)
        def _():
            halo(0).start()

    load_wave(0).wait()
    mask(0)

    @pl.when((c == 1) & (before == 1))
    def _():
        halo(1).start()

    def passed(slot):
        return pltpu.make_async_remote_copy(
            src_ref=wide.at[slot],
            dst_ref=wide.at[slot],
            send_sem=halo_send.at[2],
            recv_sem=halo_recv.at[1],
            device_id=sibling,
            device_id_type=MESH,
        )

    for s in (1, 2):
        load_wave(s).wait()
        mask(s)
    load_shift.wait()

    def to_sibling(p):
        return pltpu.make_async_remote_copy(
            src_ref=lent.at[p],
            dst_ref=sib.at[p],
            send_sem=sib_send.at[p],
            recv_sem=sib_recv.at[p],
            device_id=sibling,
            device_id_type=MESH,
        )

    def scatter(p, d):
        chunk = lax.rem(z + d, nz) * rows
        return pltpu.make_async_remote_copy(
            src_ref=packed.at[p, pl.ds(pl.multiple_of(chunk, rows), rows)],
            dst_ref=landed.at[p, c * (nz - 1) + d - 1],
            send_sem=rs_send.at[p],
            recv_sem=rs_recv.at[p],
            device_id=peer(d, p),
            device_id_type=MESH,
        )

    mine = pl.ds(pl.multiple_of(z * rows, rows), rows)

    def hand_over(p):
        return pltpu.make_async_remote_copy(
            src_ref=packed.at[p, mine],
            dst_ref=landed.at[p, 2 * (nz - 1)],
            send_sem=rs_send.at[p],
            recv_sem=rs_recv.at[p],
            device_id=sibling,
            device_id_type=MESH,
        )

    def gather(p, d):
        return pltpu.make_async_remote_copy(
            src_ref=done.at[p, z],
            dst_ref=done.at[p, z],
            send_sem=ag_send.at[p],
            recv_sem=ag_recv.at[p, d - 1],
            device_id=peer(d, p),
            device_id_type=MESH,
        )

    def gather_part(p, d, k):
        return pltpu.make_async_remote_copy(
            src_ref=done.at[p, z, k],
            dst_ref=done.at[p, z, k],
            send_sem=ag_send.at[p],
            recv_sem=ag_recv.at[p, d - 1],
            device_id=peer(d, p),
            device_id_type=MESH,
        )

    def share(p, d):
        chunk = lax.rem(z - d + nz, nz)
        return pltpu.make_async_remote_copy(
            src_ref=done.at[p, chunk],
            dst_ref=done.at[p, chunk],
            send_sem=share_send.at[p],
            recv_sem=share_recv.at[p],
            device_id=sibling,
            device_id_type=MESH,
        )

    def wait_all(ref, sem):
        pltpu.make_async_copy(ref, ref, sem).wait()

    def step(it, carry):
        p = lax.div(it, 2)
        q = lax.rem(it, 2)
        e = q * c + (1 - q) * (1 - c)
        s = sector_of(p, e)

        @pl.when(it == 2)
        def _():
            @pl.when(r * before + (1 - r) * after == 1)
            def _():
                halo(1 - r).wait_recv()

            @pl.when(r * before + (1 - r) * after == 0)
            def _():
                wide[5 - 5 * r] = jnp.zeros((order, order), jnp.bfloat16)

            passed(5 - 5 * r).start()

        @pl.when(it == 3)
        def _():
            passed(5 * r).wait_recv()

        for n in range(3):
            near[n] = wide[s + n]
        left_now, right_now = load(it)

        @pl.when(it == 0)
        def _():
            for later in range(2, 4):
                for copy in load(later):
                    copy.start()

        left_now.wait()
        right_now.wait()

        def first(k):
            return jnp.dot(
                left[it, k], near[shift_ref[k] + 1], preferred_element_type=jnp.float32
            ).astype(jnp.bfloat16)

        total, ahead = None, first(0)
        for k in range(terms):
            now, ahead = ahead, first(k + 1) if k + 1 < terms else None
            term = lax.dot_general(now, right[it, k], NT, preferred_element_type=jnp.float32)
            total = term if total is None else total + term

        @pl.when((it == 0) & (c == 0))
        def _():
            pl.semaphore_wait(ready, 1)

        @pl.when(q == 0)
        def _():
            lent[p] = total.astype(jnp.bfloat16)
            to_sibling(p).start()

        @pl.when(q == 1)
        def _():
            to_sibling(p).wait_recv()
            both = total + sib[p].astype(jnp.float32)
            part[p] = both
            packed[p] = both.astype(jnp.bfloat16)

            @pl.when((p == 0) & (c == 0))
            def _():
                pl.semaphore_wait(barrier, 2 * nz - 1)
                signal(ready, sibling)

            @pl.when((p == 0) & (c == 1))
            def _():
                pl.semaphore_wait(ready, 1)

            for d in far:
                scatter(p, d).start()

            @pl.when(c != p)
            def _():
                hand_over(p).start()

        return carry

    lax.fori_loop(0, 4, step, 0)

    def reduce(p):
        mine_now = part[p, mine]
        wait_all(landed.at[p], rs_recv.at[p])
        given = landed[p, 2 * (nz - 1)].astype(jnp.float32)
        sums = [jnp.where(p == core, mine_now, given) for core in range(2)]
        for d in range(1, nz):
            for core in range(2):
                sums[core] += landed[p, core * (nz - 1) + d - 1].astype(jnp.float32)
        for core in range(2):
            done[p, z, core] = masked(sums[core], sector_of(p, core), z * rows)
            for d in far[:3]:
                gather_part(p, d, core).start()
        for d in far[3:]:
            gather(p, d).start()
        share(p, 0).start()

    def pass_on(p):
        for d in reversed(far):
            gather(p, d).wait_recv()
            share(p, d).start()

    def place(p):
        for core in range(2):
            for n in range(nz):
                out_ref[sector_of(p, core), pl.ds(n * rows, rows)] = done[p, n, core]

    reduce(c)
    pass_on(c)

    def finish(p, carry):
        to_sibling(p).wait_send()

        @pl.when(c != p)
        def _():
            wait_all(packed.at[p], rs_send.at[p])
            wait_all(done.at[p], share_recv.at[p])

        place(p)

        @pl.when(c == p)
        def _():
            wait_all(landed.at[p, pl.ds(0, nz - 1)], rs_send.at[p])
            wait_all(done.at[p, pl.ds(0, nz - 1)], ag_send.at[p])
            wait_all(done.at[p], share_send.at[p])

        return carry

    passed(5 - 5 * r).wait_send()

    @pl.when((c == 1) & (before == 1))
    def _():
        halo(1).wait_send()

    @pl.when((c == 1) & (after == 1))
    def _():
        halo(0).wait_send()

    lax.fori_loop(0, 2, finish, 0)


def body(nsec, nz, wavefunction, sector_dims, term_shift, left_env, right_env):
    count, order, _ = wavefunction.shape
    terms = left_env.shape[0]
    rows = order // nz
    bf16, f32 = jnp.bfloat16, jnp.float32
    dma = pltpu.SemaphoreType.DMA
    hbm = pl.BlockSpec(memory_space=pltpu.HBM)
    return pl.pallas_call(
        functools.partial(kernel, nsec, nz),
        out_shape=pltpu.VMEM((count, order, order), bf16),
        in_specs=[hbm] * 5,
        out_specs=pl.BlockSpec(memory_space=pltpu.VMEM),
        scratch_shapes=[
            pltpu.VMEM((count + 2, order, order), bf16),
            pltpu.VMEM((3, order, order), bf16),
            pltpu.VMEM((count, terms, order, order), bf16),
            pltpu.VMEM((count, terms, order, order), bf16),
            pltpu.VMEM((2, order, order), f32),
            pltpu.VMEM((2, order, order), bf16),
            pltpu.VMEM((2, order, order), bf16),
            pltpu.VMEM((2, order, order), bf16),
            pltpu.VMEM((2, 2 * nz - 1, rows, order), bf16),
            pltpu.VMEM((2, nz, 2, rows, order), bf16),
            pltpu.SMEM((2, count), jnp.int32),
            pltpu.SMEM((terms,), jnp.int32),
            dma((2,)),
            dma((count,)),
            dma((count,)),
            dma((count,)),
            dma((3,)),
            dma((2,)),
            dma((2,)),
            dma((2,)),
            dma((2,)),
            dma((2,)),
            dma((2,)),
            dma((2, nz - 1)),
            dma((2,)),
            dma((2,)),
            pltpu.SemaphoreType.REGULAR,
        ],
        compiler_params=pltpu.CompilerParams(
            collective_id=0, has_side_effects=True, vmem_limit_bytes=32 << 20
        ),
    )(*(
        pltpu.with_memory_space_constraint(x, pltpu.HBM)
        for x in (sector_dims.T, term_shift, wavefunction, left_env, right_env)
    ))


def solution(mesh):
    nsec, nop = mesh.shape["sec"], mesh.shape["op"]
    return jax.shard_map(
        functools.partial(body, nsec, nop // 2),
        mesh=mesh,
        in_specs=(
            P("sec", None, None),
            P("sec", None),
            P("op"),
            P("op", "sec", None, None),
            P("op", "sec", None, None),
        ),
        out_specs=P("sec", None, None),
        check_vma=False,
    )
```
